512 devices in a mesh: gx: 32 (over x, z), gy: 16 (over y, core).
Axes of the slice: x: 4, y: 8, z: 8, core: 2. Of those that a mesh axis runs over, the one named last changes fastest.
Arguments:
- features: bfloat16 [32, 131072], P(None, ('gx', 'gy')), may hold values from -6 to 6
- offsets: bfloat16 [3, 131072], P(None, ('gx', 'gy')), may hold values from 0 to 16
- point_cell: int32 [131072], P(('gx', 'gy')), may hold values from 0 to 511
- tile_owner: int32 [1024, 4], P(('gx', 'gy')), may hold values from 0 to 15, all different within a row; in each aligned block of 2 rows (0 to 1, 2 to 3, ...) at most 2 rows name the same one
- tile_local: int32 [1024, 4], P(('gx', 'gy')), may hold values from 0 to 31
- live_count: int32 [1024], P(('gx', 'gy')), may hold values from 1 to 4
- w_first: bfloat16 [64, 3], replicated, may hold values from -3.5 to 3.5
- b_first: float32 [64], replicated, may hold values from -3 to 3
- w_second: bfloat16 [64, 64], replicated, may hold values from -0.75 to 0.75
- b_second: float32 [64], replicated, may hold values from -3 to 3
- w_third: bfloat16 [32, 64], replicated, may hold values from -0.75 to 0.75
- w_point: bfloat16 [32, 32], replicated, may hold values from -1 to 1
- b_point: float32 [32], replicated, may hold values from -3 to 3
- w_modes: bfloat16 [32, 32, 32, 2, 32, 32], P(None, 'gx', 'gy'), may hold values from -3 to 3
Outputs:
- latent_out: float32 [128, 128, 32, 128], P('gx', 'gy')
The draws below stay inside these ranges and needn't reach their ends.
Inputs may be any that keep to these rules, and one draw needn't show every extreme that they name: `tile_owner`: each row names 4 different owners; among the rows of one device no owner is named by more than 2 rows.
All inputs are finite; a program needn't handle non-finite values.
Results may differ from the reference program's by a relative error of at most 0.0015.
Values may be sent and summed in bfloat16 or wider, within the bound.
No kernel may reach another device: no remote copies, remote signals or barrier semaphores. Data moves between devices by JAX's collectives and lax.ppermute only.
A program may use at most 64 MiB of HBM per device.

```python
import math
import jax
import jax.numpy as jnp
import numpy as np
from jax import lax

C = 32
HID = 64
M = 32
NZ = 128
CX = 4
CY = 8
SPAN = 16
PB = 128
BLK_DEV = 2
LIST = 4
CAP = 2
NX = 128
NY = 128
BLOCKS = 1024
POINTS = 131072
COARSE = 512
N_GY = 16
DEVICES = 512


def draw_live_count(key, part):
    key_rows = jax.random.fold_in(key, 11)
    key_slots = jax.random.fold_in(key, 12)
    density = jax.random.randint(key_rows, (DEVICES, 1), 2, LIST + 1)
    lowest = (density + 1) // 2
    raw_draw = jax.random.randint(key_slots, (DEVICES, BLK_DEV), 0, 1 << 20)
    counts = lowest + raw_draw % (density - lowest + 1)
    return counts.reshape(BLOCKS).astype(jnp.int32)


def plant(array, key, smallest, high):
    place = [jax.random.randint(jax.random.fold_in(key, axis), (), 0, length) for axis, length in enumerate(array.shape)]
    widest = array.shape.index(max(array.shape))
    neighbour = place[:widest] + [(place[widest] + 1) % array.shape[widest]] + place[widest + 1:]
    return array.at[tuple(place)].set(smallest).at[tuple(neighbour)].set(high)


def level_of(key, dims, split, least, high):
    factor_of = 1.0
    for dim, shards_of in split:
        draws = jax.random.uniform(jax.random.fold_in(jax.random.fold_in(key, 6), dim), (shards_of,), jnp.float32, least / len(split), high / len(split))
        factor_of = factor_of * jnp.repeat(jnp.exp(draws), dims[dim] // shards_of).reshape((-1,) + (1,) * (len(dims) - 1 - dim))
    return factor_of


def routed_block(key, own, number, rows, amount, top, reach, slope):
    sequence = jax.random.permutation(key, amount)
    heavy_load, ordinary = portions_of(amount, rows * top, reach, slope, True), portions_of(amount, rows * top, reach, slope, False)
    places = jnp.arange(amount)

    def named(tallies, rotation):
        used = int((tallies > 0).sum())
        fixed = max(1, used // 4)
        passed = fixed + (places - fixed + rotation * (used - fixed)) % max(1, amount - fixed)
        return jnp.zeros((amount,), jnp.int32).at[sequence[jnp.where(places < fixed, places, passed)]].set(jnp.asarray(tallies, jnp.int32))

    tallies = jnp.where(number % 4 == 0, named(heavy_load, number // 4), named(ordinary, number - number // 4 - 1))
    mixed = jax.random.permutation(jax.random.fold_in(own, 3), amount)
    giver, taker = mixed[0:amount // 2 * 2:2], mixed[1:amount // 2 * 2:2]
    slack = jnp.minimum(tallies[giver] - 1, reach - tallies[taker]) // 2
    slack = jnp.where((giver == sequence[0]) | (taker == sequence[0]) | (tallies[taker] == 0), 0, jnp.maximum(slack, 0))
    passed = jax.random.randint(jax.random.fold_in(own, 4), (amount // 2,), 0, 1 << 20) % (slack + 1)
    tallies = tallies.at[giver].add(-passed).at[taker].add(passed)
    items = jnp.searchsorted(jnp.cumsum(tallies), jnp.arange(rows * top), side="right").astype(jnp.int32)
    table = items.reshape(top, rows).T
    table = table[jax.random.permutation(jax.random.fold_in(own, 1), rows)]
    rotation = jax.random.randint(jax.random.fold_in(own, 2), (rows, 1), 0, top)
    return jnp.take_along_axis(table, (jnp.arange(top)[None, :] + rotation) % top, axis=1)


def portions_of(count, total, reach, lean, full):
    portions = [(1 << 20) // math.isqrt(standing ** lean) + 1 for standing in range(1, count + 1)]
    largest = reach if full else min(reach, max(-(-total // count), total * portions[0] // sum(portions)))
    least = 1 if total - largest >= count - 1 else 0
    given, spare = [largest] + [least] * (count - 1), total - largest - least * (count - 1)
    while spare > 0:
        movable = [i for i in range(1, count) if given[i] < largest] or [i for i in range(1, count) if given[i] < reach]
        pool, budget = sum([portions[i] for i in movable]), spare
        for i in movable:
            extra = min(reach - given[i], max(1, budget * portions[i] // pool), spare)
            given[i] = given[i] + extra
            spare = spare - extra
    return np.array(given)


def bell_draw(stream_key, shape, spread, limit, pieces=(), kind=jnp.bfloat16):
    result = spread * jax.random.normal(stream_key, shape, jnp.float32)
    if pieces:
        result = result * level_of(stream_key, shape, pieces, -0.22, 0.18)
    return jnp.clip(result, -limit, limit).astype(kind)


def setup_inputs(seed: int = 0) -> dict:
    key_list = jax.random.split(jax.random.key(seed), 15)
    features = bell_draw(key_list[0], (C, POINTS), 1.0, 6.0, ((1, 512),))
    offsets = jnp.clip(16.0 * jax.random.uniform(key_list[1], (3, POINTS), jnp.float32) ** level_of(key_list[1], (3, POINTS), ((1, 512),), -0.2, 0.2), 0.0, 16.0).astype(jnp.bfloat16)
    point_cell = plant(jax.random.randint(key_list[2], (POINTS,), 0, COARSE), jax.random.fold_in(key_list[2], 1), 0, COARSE - 1).astype(jnp.int32)
    tile_owner_keys = jax.random.split(jax.random.fold_in(key_list[3], 1), BLOCKS // BLK_DEV)
    tile_owner_turns = jax.random.permutation(jax.random.fold_in(key_list[3], 3), BLOCKS // BLK_DEV)
    tile_owner = jax.vmap(lambda own, number: routed_block(jax.random.fold_in(key_list[3], 2), own, number, BLK_DEV, N_GY, LIST, CAP, 0))(tile_owner_keys, tile_owner_turns).reshape((BLOCKS, LIST))
    tile_local = plant(jax.random.randint(key_list[4], (BLOCKS, LIST), 0, CX * CY), jax.random.fold_in(key_list[4], 1), 0, (CX * CY) - 1).astype(jnp.int32)
    live_count = draw_live_count(jax.random.fold_in(key_list[14], 71), 0)
    w_first = bell_draw(key_list[6], (HID, 3), 3 ** -0.5, 3.5)
    b_first = bell_draw(key_list[7], (HID,), 0.5, 3.0, (), jnp.float32)
    w_second = bell_draw(key_list[8], (HID, HID), HID ** -0.5, 0.75)
    b_second = bell_draw(key_list[9], (HID,), 0.5, 3.0, (), jnp.float32)
    w_third = bell_draw(key_list[10], (C, HID), HID ** -0.5, 0.75)
    w_point = bell_draw(key_list[11], (C, C), C ** -0.5, 1.0)
    b_point = bell_draw(key_list[12], (C,), 0.5, 3.0, (), jnp.float32)
    w_modes = bell_draw(key_list[13], (M, M, M, 2, C, C), 0.5, 3.0, ((1, 32), (2, 16)))
    return {"features": features, "offsets": offsets, "point_cell": point_cell, "tile_owner": tile_owner, "tile_local": tile_local, "live_count": live_count, "w_first": w_first, "b_first": b_first, "w_second": w_second, "b_second": b_second, "w_third": w_third, "w_point": w_point, "b_point": b_point, "w_modes": w_modes}


def phase_tables(length, modes, two_sided):
    orders = jnp.arange(modes, dtype=jnp.int32)
    if two_sided:
        frequency = jnp.where(orders < modes // 2, orders, length - modes + orders)
    else:
        frequency = orders
    places = jnp.arange(length, dtype=jnp.int32)
    turns = places[:, None] * frequency[None, :] % length
    angles = turns.astype(jnp.float32) * (2.0 * math.pi / length)
    return (jnp.cos(angles), jnp.sin(angles))

def complex_table(length, modes, direction):
    cosine, sine = phase_tables(length, modes, True)
    return jnp.stack([jnp.stack([cosine, direction * sine], -1), jnp.stack([-direction * sine, cosine], -1)], 1)

def inverse_table(length, modes):
    return jnp.transpose(complex_table(length, modes, 1.0), (2, 1, 0, 3))

def real_tables(length, modes, scale):
    cosine, sine = phase_tables(length, modes, False)
    forward = jnp.stack([cosine, -sine], -1) * scale
    inverse = jnp.stack([cosine.T, -sine.T], 1) * scale
    return (forward, inverse)

def pair_sum(block_feats, block_offsets, cell_ids, cell_x, cell_y, weights, grid_dims):
    w_first, b_first, w_second, b_second, w_third = weights
    coarse_y, coarse_z, depth = grid_dims
    along_x = cell_ids // (coarse_y * coarse_z)
    along_y = cell_ids // coarse_z % coarse_y
    along_z = cell_ids % coarse_z
    places = jnp.stack([along_x, along_y, along_z]).astype(jnp.float32) * SPAN + block_offsets.astype(jnp.float32)
    column = jnp.arange(depth, dtype=jnp.int32).astype(jnp.float32)
    centres = jnp.stack([jnp.zeros_like(column) + cell_x.astype(jnp.float32), jnp.zeros_like(column) + cell_y.astype(jnp.float32), column])
    layer_one = w_first.astype(jnp.float32)
    cell_side = layer_one[:, 0:1] * centres[0:1] + layer_one[:, 1:2] * centres[1:2] + layer_one[:, 2:3] * centres[2:3]
    point_side = layer_one[:, 0:1] * places[0:1] + layer_one[:, 1:2] * places[1:2] + layer_one[:, 2:3] * places[2:3]
    inputs = cell_side[:, :, None] - point_side[:, None, :] + b_first[:, None, None]
    hidden = jnp.sin(inputs).astype(jnp.bfloat16).reshape(w_first.shape[0], -1)
    second = jnp.dot(w_second, hidden, preferred_element_type=jnp.float32) + b_second[:, None]
    second = jax.nn.gelu(second).astype(jnp.bfloat16)
    kernel = jnp.dot(w_third, second, preferred_element_type=jnp.float32).reshape(w_third.shape[0], depth, -1)
    return lax.optimization_barrier(jnp.sum(kernel * block_feats.astype(jnp.float32)[:, None, :], axis=2)) / math.sqrt(block_feats.shape[1])

def mix_modes(spectrum, w_modes):
    weights = w_modes.astype(jnp.float32)
    real_in = spectrum[..., 0, :]
    imag_in = spectrum[..., 1, :]
    real_w = weights[..., 0, :, :]
    imag_w = weights[..., 1, :, :]
    form = 'kpqi,kpqio->kpqo'
    best = lax.Precision.HIGHEST
    real_out = jnp.einsum(form, real_in, real_w, precision=best) - jnp.einsum(form, imag_in, imag_w, precision=best)
    imag_out = jnp.einsum(form, real_in, imag_w, precision=best) + jnp.einsum(form, imag_in, real_w, precision=best)
    return jnp.stack([real_out, imag_out], 3)

def fourier_layer(latent, w_point, b_point, w_modes):
    size_x, size_y, channels, depth = latent.shape
    modes = w_modes.shape[0]
    best = lax.Precision.HIGHEST
    scale = 1.0 / math.sqrt(size_x * size_y * depth)
    forward_z, inverse_z = real_tables(depth, modes, scale)
    along_z = jnp.einsum('xycz,zks->xyksc', latent, forward_z, precision=best)
    along_y = jnp.einsum('xyqrc,yrks->xkqsc', along_z, complex_table(size_y, modes, -1.0), precision=best)
    spectrum = jnp.einsum('xpqrc,xrks->kpqsc', along_y, complex_table(size_x, modes, -1.0), precision=best)
    mixed = mix_modes(spectrum, w_modes)
    back_x = jnp.einsum('kpqrc,krxs->xpqsc', mixed, inverse_table(size_x, modes), precision=best)
    back_y = jnp.einsum('xpqrc,prys->xyqsc', back_x, inverse_table(size_y, modes), precision=best)
    spectral = jnp.einsum('xyqrc,qrz->xycz', back_y, inverse_z, precision=best)
    pointwise = jnp.einsum('xycz,co->xyoz', latent, w_point.astype(jnp.float32), precision=best)
    return jax.nn.gelu(spectral + pointwise + b_point[:, None])

def reference(features, offsets, point_cell, tile_owner, tile_local, live_count, w_first, b_first, w_second, b_second, w_third, w_point, b_point, w_modes):
    weights = (w_first, b_first, w_second, b_second, w_third)
    grid_dims = (NY // SPAN, NZ // SPAN, NZ)
    block_feats = features.reshape(C, BLOCKS, PB).transpose(1, 0, 2)
    block_offsets = offsets.reshape(3, BLOCKS, PB).transpose(1, 0, 2)
    block_cells = point_cell.reshape(BLOCKS, PB)
    pair_ids = jnp.arange(BLOCKS * LIST, dtype=jnp.int32)
    block_ids = pair_ids // LIST
    slot_ids = pair_ids % LIST
    row_ids = block_ids // (BLK_DEV * N_GY)
    owners = tile_owner.reshape(-1)
    tile_slot = tile_local.reshape(-1)
    cell_x = CX * row_ids + tile_slot // CY
    cell_y = CY * owners + tile_slot % CY
    is_live = slot_ids < live_count[block_ids]

    def one_pair(pair_index):
        block_now = block_ids[pair_index]
        return lax.cond(is_live[pair_index], lambda: pair_sum(block_feats[block_now], block_offsets[block_now], block_cells[block_now], cell_x[pair_index], cell_y[pair_index], weights, grid_dims), lambda: jnp.zeros((C, NZ), jnp.float32))
    contribs = lax.map(one_pair, pair_ids)
    grid = jnp.zeros((NX * NY, C, NZ), jnp.float32).at[cell_x * NY + cell_y].add(contribs)
    latent = grid.reshape(NX, NY, C, NZ)
    return fourier_layer(latent, w_point, b_point, w_modes)
```

```python
import functools
import math

import jax
import jax.numpy as jnp
import numpy as np
from jax import lax
from jax.experimental import pallas as pl
from jax.experimental.pallas import tpu as pltpu
from jax.sharding import PartitionSpec as P

NZ = 128
CX = 4
CY = 8
SPAN = 16
PB = 128
C = 32
HID = 64
N_GX = 32
N_GY = 16
BLK = 2
LIST = 4
PAIRS = BLK * LIST
MODES = 32
UNROLL = 4
F32 = jnp.float32
BF16 = jnp.bfloat16
BEST = lax.Precision.HIGHEST
NN = (((1,), (0,)), ((), ()))
NT = (((1,), (1,)), ((), ()))
TN = (((0,), (0,)), ((), ()))
HALF_PI = (1.5703125, 4.837512969970703125e-4, 7.549789954891882e-8)
SIN_TERMS = (-1.9515295891e-4, 8.3321608736e-3, -1.6666654611e-1)
COS_TERMS = (2.443315711809948e-5, -1.388731625493765e-3, 4.166664568298827e-2)
GELU_A = math.sqrt(2.0 / math.pi)
GELU_B = GELU_A * 0.044715


def iota(shape, dim):
    return lax.broadcasted_iota(jnp.int32, shape, dim)


def dot(a, b, dims=NN):
    return lax.dot_general(a, b, dims, preferred_element_type=F32)


def fine_dot(a, b, dims=NN):
    return lax.dot_general(a, b, dims, precision=BEST, preferred_element_type=F32)


def halves(x):
    high = x.astype(BF16)
    return high, (x - high.astype(F32)).astype(BF16)


def sin_cos(x):
    count = jnp.floor(x * (2.0 / math.pi) + 0.5)
    rest = x - count * HALF_PI[0]
    rest = rest - count * HALF_PI[1]
    rest = rest - count * HALF_PI[2]
    square = rest * rest
    s = (SIN_TERMS[0] * square + SIN_TERMS[1]) * square + SIN_TERMS[2]
    s = s * square * rest + rest
    c = (COS_TERMS[0] * square + COS_TERMS[1]) * square + COS_TERMS[2]
    c = c * square * square - 0.5 * square + 1.0
    quarter = count.astype(jnp.int32)
    odd = (quarter & 1) != 0
    sine = jnp.where(odd, c, s)
    cosine = jnp.where(odd, s, c)
    sine = jnp.where((quarter & 2) != 0, -sine, sine)
    cosine = jnp.where(((quarter + 1) & 2) != 0, -cosine, cosine)
    return sine, cosine


def angles(length, two_sided):
    orders = np.arange(MODES)
    frequency = np.where(orders < MODES // 2, orders, length - MODES + orders) if two_sided else orders
    turns = np.arange(length)[:, None] * frequency[None, :] % length
    return turns * (2.0 * math.pi / length)


def f32(x):
    return np.ascontiguousarray(x, dtype=np.float32)


def split_table(x):
    high = f32(x).astype(jnp.bfloat16)
    low = (x - high.astype(np.float64)).astype(np.float32).astype(jnp.bfloat16)
    return high, low


def tables(size_x, size_y):
    scale = 1.0 / math.sqrt(size_x * size_y * NZ)
    along_z = angles(NZ, False)
    both = np.stack([np.cos(along_z), -np.sin(along_z)], -1) * scale
    both = both.reshape(NZ, N_GY, 4)
    forward_z = f32(both.transpose(2, 1, 0).reshape(4 * N_GY, NZ))
    inverse_z = np.concatenate(split_table(both.reshape(NZ, 4 * N_GY).T), 1)
    along_y = angles(size_y, True)
    per_row = np.repeat(along_y.T, CX, axis=0)
    phase_y = np.concatenate(split_table(np.cos(per_row)) + split_table(np.sin(per_row)), 0)
    back_y = f32(np.concatenate([np.cos(along_y), np.sin(along_y)], 1))
    along_x = angles(size_x, True)
    forward_x = f32(np.concatenate([np.cos(along_x), np.sin(along_x)], 0).T.reshape(MODES, 2 * size_x))
    back_x = f32(np.concatenate([np.cos(along_x), np.sin(along_x)], 1))
    return forward_z, inverse_z, phase_y, back_y, forward_x, back_x


def pair_kernel(
    owner, tile, live, feats, offs, cells, rows, w2, w3, wp, fz,
    modes_out, cells_out,
    cz, sz, w2b, w3b, side, point, feat, sin_p, cos_p, sums, held,
):
    gx = lax.axis_index("gx")
    gy = lax.axis_index("gy")
    pick = ((iota((4 * HID, HID), 0) & (HID - 1)) == iota((4 * HID, HID), 1)).astype(BF16)
    spread = dot(dot(pick, w2[...], NT).astype(BF16), pick, NT)
    same = (iota(spread.shape, 0) // HID) == (iota(spread.shape, 1) // HID)
    w2b[...] = jnp.where(same, spread, 0.0).astype(BF16)
    pick_c = ((iota((4 * C, C), 0) & (C - 1)) == iota((4 * C, C), 1)).astype(BF16)
    spread = dot(dot(pick, w3[...], NT).astype(BF16), pick_c, NT)
    same = (iota(spread.shape, 0) // HID) == (iota(spread.shape, 1) // C)
    w3b[...] = jnp.where(same, 0.5 * spread, 0.0).astype(BF16)
    side[...] = fine_dot(rows[...], pick.astype(F32), NT)
    cell_z = ((iota((NZ // 4, 4 * HID), 1) // HID) * (NZ // 4) + iota((NZ // 4, 4 * HID), 0)).astype(F32)
    sine, cosine = sin_cos(side[2:3, :] * cell_z)
    cz[...] = cosine
    sz[...] = sine
    sums[...] = jnp.zeros_like(sums)
    cells_out[...] = jnp.zeros_like(cells_out)
    row_of = iota((PB, PB), 0)
    for b in range(BLK):
        span = slice(b * PB, (b + 1) * PB)
        q = cells[:, span]
        place = [
            ((q // 64) * SPAN).astype(F32) + offs[0:1, span].astype(F32),
            ((q // 8 % 8) * SPAN).astype(F32) + offs[1:2, span].astype(F32),
            ((q % 8) * SPAN).astype(F32) + offs[2:3, span].astype(F32),
        ]
        stack = jnp.where(row_of == 0, place[0], jnp.where(row_of == 1, place[1], place[2]))
        turned = jnp.transpose(stack)
        point[b] = (
            turned[:, 0:1] * side[0:1, :PB] + turned[:, 1:2] * side[1:2, :PB] + turned[:, 2:3] * side[2:3, :PB]
        )
        block = feats[:, span].astype(F32) * (1.0 / math.sqrt(PB))
        feat[b] = jnp.transpose(jnp.concatenate([block] * 4, axis=0))
    for b in range(BLK):

        def one_pair(s, carry, b=b):
            t = tile[b, s]
            x = (CX * gx + t // CY).astype(F32)
            y = (CY * owner[b, s] + t % CY).astype(F32)
            line = side[0:1, :PB] * x + side[1:2, :PB] * y + side[3:4, :PB]
            sine, cosine = sin_cos(line - point[b])
            sin_p[...] = sine
            cos_p[...] = cosine

            def some_cells(i, carry):
                for u in range(UNROLL):
                    g = i * UNROLL + u
                    c = cz[pl.ds(g, 1), :]
                    d = sz[pl.ds(g, 1), :]
                    sp = sin_p[...]
                    cp = cos_p[...]
                    first = jnp.concatenate(
                        [sp * c[:, :PB] + cp * d[:, :PB], sp * c[:, PB:] + cp * d[:, PB:]], axis=1
                    ).astype(BF16)
                    h = dot(first, w2b[...]) + side[4:5, :]
                    th = jnp.tanh(h * (GELU_B * (h * h) + GELU_A))
                    second = (h + h * th).astype(BF16)
                    kern = dot(second, w3b[...])
                    total = jnp.sum(kern * feat[b], axis=0, keepdims=True)
                    sums[pl.ds((b * LIST + s) * (NZ // 4) + g, 1), :] = total
                return carry

            lax.fori_loop(0, NZ // 4 // UNROLL, some_cells, 0)
            return carry

        lax.fori_loop(0, live[b], one_pair, 0)
    shape = (4 * C, 16 * C)
    copy_c = (
        ((iota(shape, 0) & (C - 1)) == (iota(shape, 1) & (C - 1))) & ((iota(shape, 0) // C) == (iota(shape, 1) // (4 * C)))
    ).astype(BF16)
    high, low = halves(sums[...])
    wide = dot(high, copy_c) + dot(low, copy_c)
    by_cell = [
        jnp.concatenate([wide[j * 32 : (j + 1) * 32, k * 128 : (k + 1) * 128] for k in range(4)], axis=0)
        for j in range(PAIRS)
    ]
    eye = (iota((C, 4 * C), 0) == iota((C, 4 * C), 1)).astype(BF16)
    wpt = dot(wp[...], eye, TN).astype(BF16)
    lane_group = iota((N_GY, 4 * C), 1) // C
    held[...] = jnp.zeros_like(held)
    for j in range(PAIRS):
        b, s = divmod(j, LIST)
        full = fine_dot(fz[...], by_cell[j])
        picked = jnp.zeros((N_GY, 4 * C), F32)
        for g in range(4):
            picked = jnp.where(lane_group == g, full[g * N_GY : (g + 1) * N_GY], picked)
        held[:, j, :] = picked
        high, low = halves(by_cell[j])
        mapped = dot(wpt, high, NT) + dot(wpt, low, NT)

        @pl.when(s < live[b])
        def _(b=b, s=s, mapped=mapped):
            cells_out[owner[b, s], b * C : (b + 1) * C, :] = mapped.astype(cells_out.dtype)

    lane = iota((1, 128), 1)
    xs = jnp.zeros((1, 128), jnp.int32)
    ys = jnp.zeros((1, 128), jnp.int32)
    on = jnp.zeros((1, 128), jnp.int32)
    for j in range(PAIRS):
        b, s = divmod(j, LIST)
        here = lane == gy * PAIRS + j
        t = tile[b, s]
        xs = jnp.where(here, t // CY, xs)
        ys = jnp.where(here, CY * owner[b, s] + t % CY, ys)
        on = jnp.where(here & (s < live[b]), 1, on)
    for k, v in enumerate((xs, ys, on)):
        held[:, PAIRS + k, :] = jnp.broadcast_to(v.astype(F32), (N_GY, 128))
    modes_out[...] = held[...].astype(modes_out.dtype)


def y_kernel(got, phase, out, slots):
    gy = lax.axis_index("gy")
    full = got[...].astype(F32)
    values = full[:, :PAIRS, :].reshape(N_GY * PAIRS, 128)
    extra = full[:, PAIRS:, :]
    sent = jnp.sum(extra, axis=0)
    xs, ys, on = sent[0:1], sent[1:2], sent[2:3]
    square = (128, 128)
    hot = ((iota(square, 0).astype(F32) == ys) & (on > 0.5)).astype(BF16)
    turned = dot(phase[...], hot)
    here = (iota(square, 0) & (CX - 1)).astype(F32) == xs
    cosine = jnp.where(here, turned[0:128] + turned[128:256], 0.0)
    sine = jnp.where(here, turned[256:384] + turned[384:512], 0.0)
    result = fine_dot(cosine, values) + fine_dot(sine, rotated(values, 1.0))
    out[...] = result.reshape(MODES, CX, 128).astype(out.dtype)
    yi = ys.astype(jnp.int32)
    mine = ((yi // CY) == gy) & (on > 0.5)
    number = jnp.where(mine, xs.astype(jnp.int32) * CY + (yi & (CY - 1)) + 1, 0).astype(BF16)
    group = ((iota(square, 0) // LIST) == iota(square, 1)).astype(BF16)
    slots[...] = dot(jnp.broadcast_to(number, (8, 128)), group).astype(jnp.int32) - 1


def rotated(x, sign):
    up = pltpu.roll(x, 128 - C, 1)
    down = pltpu.roll(x, C, 1)
    real = ((iota(x.shape, 1) // C) & 1) == 0
    return jnp.where(real, sign * up, -sign * down)


def x_kernel(got, weights, forward, back, out):
    size_x = CX * N_GX
    values = got[...].astype(F32).reshape(size_x, 128)
    spectrum = fine_dot(forward[:, :size_x], values) + fine_dot(forward[:, size_x:], rotated(values, 1.0))
    parts = [spectrum if g == 0 else pltpu.roll(spectrum, 128 - g * C, 1) for g in range(4)]
    high, low = halves(jnp.concatenate(parts, axis=0))
    spread = ((iota((128, C * C), 1) // C) == iota((128, C * C), 0)).astype(BF16)
    wide = dot(high, spread) + dot(low, spread)
    totals = []
    for k in range(2):
        real = wide[(2 * k) * MODES : (2 * k + 1) * MODES]
        imag = wide[(2 * k + 1) * MODES : (2 * k + 2) * MODES]
        sum_r = jnp.zeros((MODES, 128), F32)
        sum_i = jnp.zeros((MODES, 128), F32)
        for j in range(C * C // 128):
            lanes = slice(j * 128, (j + 1) * 128)
            at = (2 * k) * C * C + j * 128
            wr = weights[:, at : at + 128].astype(F32)
            wi = weights[:, at + C * C : at + C * C + 128].astype(F32)
            sum_r = sum_r + real[:, lanes] * wr - imag[:, lanes] * wi
            sum_i = sum_i + real[:, lanes] * wi + imag[:, lanes] * wr
        for v in (sum_r, sum_i):
            v = v + pltpu.roll(v, 64, 1)
            totals.append(v + pltpu.roll(v, 32, 1))
    group = iota((MODES, 128), 1) // C
    r0, i0, r1, i1 = totals
    mixed = jnp.where(group == 0, r0, jnp.where(group == 1, i0, jnp.where(group == 2, r1, i1)))
    other = jnp.where(group == 0, -i0, jnp.where(group == 1, r0, jnp.where(group == 2, -i1, r1)))
    result = fine_dot(back[...], jnp.concatenate([mixed, other], axis=0))
    out[...] = result.reshape(N_GX, CX, 128).astype(out.dtype)


def back_kernel(got, back, out):
    lines = [got[:, x, :].astype(F32) for x in range(CX)]
    group = iota((MODES, 128), 1) // C
    turned = []
    for g in range(4):
        line = jnp.zeros((MODES, 128), F32)
        for x in range(CX):
            shift = ((x - g) * C) % 128
            moved = lines[x] if shift == 0 else pltpu.roll(lines[x], shift, 1)
            line = jnp.where(group == x, moved, line)
        turned.append(line)
    size_y = CY * N_GY
    for k in range(2):
        real, imag = turned[2 * k], turned[2 * k + 1]
        stack = jnp.concatenate(
            [jnp.concatenate([real, imag], axis=1), jnp.concatenate([-imag, real], axis=1)], axis=0
        )
        result = fine_dot(back[...], stack)
        for g in range(2):
            piece = result[:, g * 128 : (g + 1) * 128].reshape(N_GY, CY, 128)
            at = (2 * k + g) * CY
            out[:, at : at + CY, :] = piece.astype(out.dtype)


def end_kernel(slots, got, cells, inverse, bias, out, wide, total):
    wide[...] = got[...].astype(F32).reshape(N_GY * 4 * CY, 128)
    column = jnp.broadcast_to(bias[...], (C, NZ))
    for y in range(CY):
        values = wide[pl.ds(y, 4 * N_GY, stride=CY), :].astype(BF16)
        both = dot(values, inverse[...], TN)
        line = both[:, :NZ] + both[:, NZ:]
        for x in range(CX):
            total[x * CY + y] = line[x * C : (x + 1) * C] + column
    for n in range(N_GY * BLK):
        src, b = divmod(n, BLK)
        t = slots[0, n]

        @pl.when(t >= 0)
        def _(src=src, b=b, t=t):
            total[t] = total[t] + cells[src, b * C : (b + 1) * C, :].astype(F32)

    for t in range(CX * CY):
        h = total[t]
        th = jnp.tanh(h * (GELU_B * (h * h) + GELU_A))
        out[t // CY, t % CY] = 0.5 * (h + h * th)


def call(kernel, out_shape, in_specs, scratch=(), flops=0, size=0):
    return pl.pallas_call(
        kernel,
        out_shape=out_shape,
        in_specs=in_specs,
        scratch_shapes=list(scratch),
        compiler_params=pltpu.CompilerParams(vmem_limit_bytes=40 * 1024 * 1024),
        cost_estimate=pl.CostEstimate(flops=flops, bytes_accessed=size, transcendentals=0),
    )


VM = pl.BlockSpec(memory_space=pltpu.VMEM)
SM = pl.BlockSpec(memory_space=pltpu.SMEM)


def local(
    features, offsets, point_cell, tile_owner, tile_local, live_count,
    w_first, b_first, w_second, b_second, w_third, w_point, b_point, w_modes,
):
    forward_z, inverse_z, phase_y, back_y, forward_x, back_x = tables(CX * N_GX, CY * N_GY)
    rows = jnp.concatenate(
        [w_first.astype(F32).T, b_first[None], b_second[None], jnp.zeros((3, HID), F32)], axis=0
    )
    vm = pltpu.VMEM
    modes, mapped = call(
        pair_kernel,
        (
            jax.ShapeDtypeStruct((N_GY, 16, 128), BF16),
            jax.ShapeDtypeStruct((N_GY, BLK * C, NZ), BF16),
        ),
        [SM, SM, SM] + [VM] * 8,
        [
            vm((NZ // 4, 4 * HID), F32), vm((NZ // 4, 4 * HID), F32),
            vm((4 * HID, 4 * HID), BF16), vm((4 * HID, 4 * C), BF16),
            vm((8, 4 * HID), F32), vm((BLK, PB, PB), F32), vm((BLK, PB, PB), F32),
            vm((PB, PB), F32), vm((PB, PB), F32),
            vm((PAIRS * NZ // 4, 4 * C), F32), vm((N_GY, 16, 128), F32),
        ],
        flops=1_600_000_000, size=1_000_000,
    )(
        tile_owner, tile_local, live_count, features, offsets, point_cell.reshape(1, -1),
        rows, w_second, w_third, w_point, forward_z,
    )
    modes = lax.all_to_all(modes, "gy", 0, 0, tiled=True)
    mapped = lax.all_to_all(mapped, "gy", 0, 0, tiled=True)
    along_y, slots = call(
        y_kernel,
        (jax.ShapeDtypeStruct((MODES, CX, 128), F32), jax.ShapeDtypeStruct((8, 128), jnp.int32)),
        [VM, VM],
        flops=100_000_000, size=500_000,
    )(modes, phase_y)
    along_y = lax.all_to_all(along_y, "gx", 0, 0, tiled=True)
    lines = call(
        x_kernel,
        jax.ShapeDtypeStruct((N_GX, CX, 128), F32),
        [VM] * 4,
        flops=100_000_000, size=500_000,
    )(along_y, w_modes.reshape(MODES, -1), forward_x, back_x)
    lines = lax.all_to_all(lines, "gx", 0, 0, tiled=True)
    cells = call(
        back_kernel,
        jax.ShapeDtypeStruct((N_GY, 4 * CY, 128), BF16),
        [VM] * 2,
        flops=100_000_000, size=500_000,
    )(lines, back_y)
    cells = lax.all_to_all(cells, "gy", 0, 0, tiled=True)
    return call(
        end_kernel,
        jax.ShapeDtypeStruct((CX, CY, C, NZ), F32),
        [SM] + [VM] * 4,
        [vm((N_GY * 4 * CY, 128), F32), vm((CX * CY, C, NZ), F32)],
        flops=100_000_000, size=1_000_000,
    )(slots, cells, mapped, inverse_z, b_point.reshape(C, 1))


def solution(mesh):
    both = ("gx", "gy")
    return jax.shard_map(
        local,
        mesh=mesh,
        in_specs=(
            P(None, both), P(None, both), P(both), P(both, None), P(both, None), P(both),
            P(), P(), P(), P(), P(), P(), P(),
            P(None, "gx", "gy", None, None, None),
        ),
        out_specs=P("gx", "gy", None, None),
        check_vma=False,
    )
```

```python
import functools
import math

import jax
import jax.numpy as jnp
import numpy as np
from jax import lax
from jax.experimental import pallas as pl
from jax.experimental.pallas import tpu as pltpu
from jax.sharding import PartitionSpec as P

NZ = 128
CX = 4
CY = 8
SPAN = 16
PB = 128
C = 32
HID = 64
N_GX = 32
N_GY = 16
BLK = 2
LIST = 4
PAIRS = BLK * LIST
MODES = 32
UNROLL = 1
STACK = 32
VMEM_ONE = 62 * 1024 * 1024
F32 = jnp.float32
BF16 = jnp.bfloat16
BEST = lax.Precision.HIGHEST
NN = (((1,), (0,)), ((), ()))
NT = (((1,), (1,)), ((), ()))
TN = (((0,), (0,)), ((), ()))
HALF_PI = (1.5703125, 4.837512969970703125e-4, 7.549789954891882e-8)
SIN_TERMS = (-1.9515295891e-4, 8.3321608736e-3, -1.6666654611e-1)
COS_TERMS = (2.443315711809948e-5, -1.388731625493765e-3, 4.166664568298827e-2)
GELU_A = math.sqrt(2.0 / math.pi)
GELU_B = GELU_A * 0.044715


def iota(shape, dim):
    return lax.broadcasted_iota(jnp.int32, shape, dim)


def dot(a, b, dims=NN):
    return lax.dot_general(a, b, dims, preferred_element_type=F32)


def fine_dot(a, b, dims=NN):
    return lax.dot_general(a, b, dims, precision=BEST, preferred_element_type=F32)


def halves(x):
    high = x.astype(BF16)
    return high, (x - high.astype(F32)).astype(BF16)


def sin_cos(x):
    count = jnp.floor(x * (2.0 / math.pi) + 0.5)
    rest = x - count * HALF_PI[0]
    rest = rest - count * HALF_PI[1]
    rest = rest - count * HALF_PI[2]
    square = rest * rest
    s = (SIN_TERMS[0] * square + SIN_TERMS[1]) * square + SIN_TERMS[2]
    s = s * square * rest + rest
    c = (COS_TERMS[0] * square + COS_TERMS[1]) * square + COS_TERMS[2]
    c = c * square * square - 0.5 * square + 1.0
    quarter = count.astype(jnp.int32)
    odd = (quarter & 1) != 0
    sine = jnp.where(odd, c, s)
    cosine = jnp.where(odd, s, c)
    sine = jnp.where((quarter & 2) != 0, -sine, sine)
    cosine = jnp.where(((quarter + 1) & 2) != 0, -cosine, cosine)
    return sine, cosine


def angles(length, two_sided):
    orders = np.arange(MODES)
    frequency = np.where(orders < MODES // 2, orders, length - MODES + orders) if two_sided else orders
    turns = np.arange(length)[:, None] * frequency[None, :] % length
    return turns * (2.0 * math.pi / length)


def f32(x):
    return np.ascontiguousarray(x, dtype=np.float32)


def split_table(x):
    high = f32(x).astype(jnp.bfloat16)
    low = (x - high.astype(np.float64)).astype(np.float32).astype(jnp.bfloat16)
    return high, low


def tables(size_x, size_y):
    scale = 1.0 / math.sqrt(size_x * size_y * NZ)
    along_z = angles(NZ, False)
    both = np.stack([np.cos(along_z), -np.sin(along_z)], -1) * scale
    both = both.reshape(NZ, N_GY, 4)
    forward_z = np.concatenate(split_table(both.transpose(2, 1, 0).reshape(4 * N_GY, NZ)), 0)
    inverse_z = np.concatenate(split_table(both.reshape(NZ, 4 * N_GY).T), 1)
    along_y = angles(size_y, True)
    per_row = np.repeat(along_y.T, CX, axis=0)
    phase_y = np.concatenate(split_table(np.cos(per_row)) + split_table(np.sin(per_row)), 0)
    back_y = f32(np.concatenate([np.cos(along_y), np.sin(along_y)], 1))
    along_x = angles(size_x, True)
    forward_x = f32(np.concatenate([np.cos(along_x), np.sin(along_x)], 0).T.reshape(MODES, 2 * size_x))
    back_x = f32(np.concatenate([np.cos(along_x), np.sin(along_x)], 1))
    return forward_z, inverse_z, phase_y, back_y, forward_x, back_x


def pair_kernel(
    owner, tile, live, feats, offs, cells, w1, b1, b2, w2, w3, fz,
    modes_out, sums,
    cz, sz, w2b, w3b, side, point, feat, sin_p, cos_p, held,
):
    gx = lax.axis_index("gx")
    gy = lax.axis_index("gy")
    pick = ((iota((4 * HID, HID), 0) & (HID - 1)) == iota((4 * HID, HID), 1)).astype(BF16)
    spread = dot(dot(pick, w2[...], NT).astype(BF16), pick, NT)
    same = (iota(spread.shape, 0) // HID) == (iota(spread.shape, 1) // HID)
    w2b[...] = jnp.where(same, spread, 0.0).astype(BF16)
    pick_c = ((iota((4 * C, C), 0) & (C - 1)) == iota((4 * C, C), 1)).astype(BF16)
    spread = dot(dot(pick, w3[...], NT).astype(BF16), pick_c, NT)
    same = (iota(spread.shape, 0) // HID) == (iota(spread.shape, 1) // C)
    w3b[...] = jnp.where(same, 0.5 * spread, 0.0).astype(BF16)
    shape = (HID, 4 * HID)
    pick_t = (iota(shape, 0) == (iota(shape, 1) & (HID - 1))).astype(F32)
    side[0:3, :] = fine_dot(w1[...].astype(F32), pick_t)
    side[3:4, :] = fine_dot(jnp.broadcast_to(b1[...], (8, HID)), pick_t)[0:1]
    side[4:5, :] = fine_dot(jnp.broadcast_to(b2[...], (8, HID)), pick_t)[0:1]
    cell_z = ((iota((NZ // 4, 4 * HID), 1) // HID) * (NZ // 4) + iota((NZ // 4, 4 * HID), 0)).astype(F32)
    sine, cosine = sin_cos(side[2:3, :] * cell_z)
    cz[...] = cosine
    sz[...] = sine
    sums[...] = jnp.zeros_like(sums)
    row_of = iota((PB, PB), 0)
    for b in range(BLK):
        span = slice(b * PB, (b + 1) * PB)
        q = cells[:, span]
        place = [
            ((q // 64) * SPAN).astype(F32) + offs[0:1, span].astype(F32),
            ((q // 8 % 8) * SPAN).astype(F32) + offs[1:2, span].astype(F32),
            ((q % 8) * SPAN).astype(F32) + offs[2:3, span].astype(F32),
        ]
        stack = jnp.where(row_of == 0, place[0], jnp.where(row_of == 1, place[1], place[2]))
        turned = jnp.transpose(stack)
        point[b] = (
            turned[:, 0:1] * side[0:1, :PB] + turned[:, 1:2] * side[1:2, :PB] + turned[:, 2:3] * side[2:3, :PB]
        )
        block = feats[:, span].astype(F32) * (1.0 / math.sqrt(PB))
        feat[b] = jnp.transpose(jnp.concatenate([block] * 4, axis=0))
    for b in range(BLK):

        def one_pair(s, carry, b=b):
            t = tile[b, s]
            x = (CX * gx + t // CY).astype(F32)
            y = (CY * owner[b, s] + t % CY).astype(F32)
            line = side[0:1, :PB] * x + side[1:2, :PB] * y + side[3:4, :PB]
            sine, cosine = sin_cos(line - point[b])
            sin_p[...] = sine
            cos_p[...] = cosine

            def some_cells(i, carry):
                for u in range(UNROLL):
                    g = (i * UNROLL + u) * STACK
                    sp = sin_p[...]
                    cp = cos_p[...]
                    lines = []
                    for k in range(STACK):
                        c = cz[pl.ds(g + k, 1), :]
                        d = sz[pl.ds(g + k, 1), :]
                        lines.append(
                            jnp.concatenate(
                                [sp * c[:, :PB] + cp * d[:, :PB], sp * c[:, PB:] + cp * d[:, PB:]], axis=1
                            ).astype(BF16)
                        )
                    h = dot(jnp.concatenate(lines, axis=0), w2b[...]) + side[4:5, :]
                    th = jnp.tanh(h * (GELU_B * (h * h) + GELU_A))
                    second = (h + h * th).astype(BF16)
                    kern = dot(second, w3b[...])
                    for k in range(STACK):
                        total = jnp.sum(kern[k * PB : (k + 1) * PB] * feat[b], axis=0, keepdims=True)
                        sums[pl.ds((b * LIST + s) * (NZ // 4) + g + k, 1), :] = total
                return carry

            lax.fori_loop(0, NZ // 4 // (UNROLL * STACK), some_cells, 0)
            return carry

        lax.fori_loop(0, live[b], one_pair, 0)
    by_cell = spread_cells(sums[...])
    lane_group = iota((N_GY, 4 * C), 1) // C
    held[...] = jnp.zeros_like(held)
    table = fz[...]
    for j in range(PAIRS):
        high, low = by_cell[0][j], by_cell[1][j]
        both = dot(table, high)
        full = both[: 4 * N_GY] + both[4 * N_GY :] + dot(table[: 4 * N_GY], low)
        picked = jnp.zeros((N_GY, 4 * C), F32)
        for g in range(4):
            picked = jnp.where(lane_group == g, full[g * N_GY : (g + 1) * N_GY], picked)
        held[:, j, :] = picked
    lane = iota((1, 128), 1)
    xs = jnp.zeros((1, 128), jnp.int32)
    ys = jnp.zeros((1, 128), jnp.int32)
    on = jnp.zeros((1, 128), jnp.int32)
    for j in range(PAIRS):
        b, s = divmod(j, LIST)
        here = lane == gy * PAIRS + j
        t = tile[b, s]
        xs = jnp.where(here, t // CY, xs)
        ys = jnp.where(here, CY * owner[b, s] + t % CY, ys)
        on = jnp.where(here & (s < live[b]), 1, on)
    for k, v in enumerate((xs, ys, on)):
        held[:, PAIRS + k, :] = jnp.broadcast_to(v.astype(F32), (N_GY, 128))
    modes_out[...] = held[...].astype(modes_out.dtype)


def spread_cells(sums):
    shape = (4 * C, 16 * C)
    copy_c = (
        ((iota(shape, 0) & (C - 1)) == (iota(shape, 1) & (C - 1))) & ((iota(shape, 0) // C) == (iota(shape, 1) // (4 * C)))
    ).astype(BF16)
    terms = []
    for term in halves(sums):
        wide = dot(term, copy_c).astype(BF16)
        terms.append(
            [
                jnp.concatenate([wide[j * 32 : (j + 1) * 32, k * 128 : (k + 1) * 128] for k in range(4)], axis=0)
                for j in range(PAIRS)
            ]
        )
    return terms


def map_kernel(owner, live, sums, wp, out):
    high, low = spread_cells(sums[...])
    eye = (iota((C, 4 * C), 0) == iota((C, 4 * C), 1)).astype(BF16)
    wpt = dot(wp[...], eye, TN).astype(BF16)
    out[...] = jnp.zeros_like(out)
    for j in range(PAIRS):
        b, s = divmod(j, LIST)
        mapped = dot(wpt, high[j], NT) + dot(wpt, low[j], NT)

        @pl.when(s < live[b])
        def _(b=b, s=s, mapped=mapped):
            out[owner[b, s], b * C : (b + 1) * C, :] = mapped.astype(out.dtype)


def y_kernel(got, phase, out, slots):
    gy = lax.axis_index("gy")
    full = got[...].astype(F32)
    values = full[:, :PAIRS, :].reshape(N_GY * PAIRS, 128)
    extra = full[:, PAIRS:, :]
    sent = jnp.sum(extra, axis=0)
    xs, ys, on = sent[0:1], sent[1:2], sent[2:3]
    square = (128, 128)
    hot = ((iota(square, 0).astype(F32) == ys) & (on > 0.5)).astype(BF16)
    turned = dot(phase[...], hot)
    here = (iota(square, 0) & (CX - 1)).astype(F32) == xs
    cosine = jnp.where(here, turned[0:128] + turned[128:256], 0.0)
    sine = jnp.where(here, turned[256:384] + turned[384:512], 0.0)
    result = fine_dot(cosine, values) + fine_dot(sine, rotated(values, 1.0))
    out[...] = result.reshape(MODES, CX, 128).astype(out.dtype)
    yi = ys.astype(jnp.int32)
    mine = ((yi // CY) == gy) & (on > 0.5)
    number = jnp.where(mine, xs.astype(jnp.int32) * CY + (yi & (CY - 1)) + 1, 0).astype(BF16)
    group = ((iota(square, 0) // LIST) == iota(square, 1)).astype(BF16)
    slots[...] = dot(jnp.broadcast_to(number, (8, 128)), group).astype(jnp.int32) - 1


def rotated(x, sign):
    up = pltpu.roll(x, 128 - C, 1)
    down = pltpu.roll(x, C, 1)
    real = ((iota(x.shape, 1) // C) & 1) == 0
    return jnp.where(real, sign * up, -sign * down)


def x_kernel(got, weights, forward, back, out):
    size_x = CX * N_GX
    values = got[...].astype(F32).reshape(size_x, 128)
    spectrum = fine_dot(forward[:, :size_x], values) + fine_dot(forward[:, size_x:], rotated(values, 1.0))
    parts = [spectrum if g == 0 else pltpu.roll(spectrum, 128 - g * C, 1) for g in range(4)]
    high, low = halves(jnp.concatenate(parts, axis=0))
    spread = ((iota((128, C * C), 1) // C) == iota((128, C * C), 0)).astype(BF16)
    wide = dot(high, spread) + dot(low, spread)
    totals = []
    for k in range(2):
        real = wide[(2 * k) * MODES : (2 * k + 1) * MODES]
        imag = wide[(2 * k + 1) * MODES : (2 * k + 2) * MODES]
        sum_r = jnp.zeros((MODES, 128), F32)
        sum_i = jnp.zeros((MODES, 128), F32)
        for j in range(C * C // 128):
            lanes = slice(j * 128, (j + 1) * 128)
            at = (2 * k) * C * C + j * 128
            wr = weights[:, at : at + 128].astype(F32)
            wi = weights[:, at + C * C : at + C * C + 128].astype(F32)
            sum_r = sum_r + real[:, lanes] * wr - imag[:, lanes] * wi
            sum_i = sum_i + real[:, lanes] * wi + imag[:, lanes] * wr
        for v in (sum_r, sum_i):
            v = v + pltpu.roll(v, 64, 1)
            totals.append(v + pltpu.roll(v, 32, 1))
    group = iota((MODES, 128), 1) // C
    r0, i0, r1, i1 = totals
    mixed = jnp.where(group == 0, r0, jnp.where(group == 1, i0, jnp.where(group == 2, r1, i1)))
    other = jnp.where(group == 0, -i0, jnp.where(group == 1, r0, jnp.where(group == 2, -i1, r1)))
    result = fine_dot(back[...], jnp.concatenate([mixed, other], axis=0))
    out[...] = result.reshape(N_GX, CX, 128).astype(out.dtype)


def back_kernel(got, back, held, out):
    out[:, 4 * CY :, :] = held[...]
    lines = [got[:, x, :].astype(F32) for x in range(CX)]
    group = iota((MODES, 128), 1) // C
    turned = []
    for g in range(4):
        line = jnp.zeros((MODES, 128), F32)
        for x in range(CX):
            shift = ((x - g) * C) % 128
            moved = lines[x] if shift == 0 else pltpu.roll(lines[x], shift, 1)
            line = jnp.where(group == x, moved, line)
        turned.append(line)
    size_y = CY * N_GY
    for k in range(2):
        real, imag = turned[2 * k], turned[2 * k + 1]
        stack = jnp.concatenate(
            [jnp.concatenate([real, imag], axis=1), jnp.concatenate([-imag, real], axis=1)], axis=0
        )
        result = fine_dot(back[...], stack)
        for g in range(2):
            piece = result[:, g * 128 : (g + 1) * 128].reshape(N_GY, CY, 128)
            at = (2 * k + g) * CY
            out[:, at : at + CY, :] = piece.astype(out.dtype)


def end_kernel(slots, got, inverse, bias, out, wide, total):
    wide[...] = got[:, : 4 * CY, :].astype(F32).reshape(N_GY * 4 * CY, 128)
    column = jnp.broadcast_to(bias[...], (C, NZ))
    for y in range(CY):
        values = wide[pl.ds(y, 4 * N_GY, stride=CY), :].astype(BF16)
        both = dot(values, inverse[...], TN)
        line = both[:, :NZ] + both[:, NZ:]
        for x in range(CX):
            total[x * CY + y] = line[x * C : (x + 1) * C] + column
    for n in range(N_GY * BLK):
        src, b = divmod(n, BLK)
        t = slots[0, n]

        @pl.when(t >= 0)
        def _(src=src, b=b, t=t):
            at = 4 * CY + b * C
            total[t] = total[t] + got[src, at : at + C, :].astype(F32)

    for t in range(CX * CY):
        h = total[t]
        th = jnp.tanh(h * (GELU_B * (h * h) + GELU_A))
        out[t // CY, t % CY] = 0.5 * (h + h * th)


def call(kernel, out_shape, in_specs, scratch=(), flops=0, size=0, vmem=40 * 1024 * 1024):
    return pl.pallas_call(
        kernel,
        out_shape=out_shape,
        in_specs=in_specs,
        scratch_shapes=list(scratch),
        compiler_params=pltpu.CompilerParams(vmem_limit_bytes=vmem),
        cost_estimate=pl.CostEstimate(flops=flops, bytes_accessed=size, transcendentals=0),
    )


VM = pl.BlockSpec(memory_space=pltpu.VMEM)
SM = pl.BlockSpec(memory_space=pltpu.SMEM)


def stage_one(
    features, offsets, point_cell, tile_owner, tile_local, live_count,
    w_first, b_first, w_second, b_second, w_third, *_,
):
    forward_z = tables(CX * N_GX, CY * N_GY)[0]
    vm = pltpu.VMEM
    return call(
        pair_kernel,
        (
            jax.ShapeDtypeStruct((N_GY, 16, 128), BF16),
            jax.ShapeDtypeStruct((PAIRS * NZ // 4, 4 * C), F32),
        ),
        [SM, SM, SM] + [VM] * 9,
        [
            vm((NZ // 4, 4 * HID), F32), vm((NZ // 4, 4 * HID), F32),
            vm((4 * HID, 4 * HID), BF16), vm((4 * HID, 4 * C), BF16),
            vm((8, 4 * HID), F32), vm((BLK, PB, PB), F32), vm((BLK, PB, PB), F32),
            vm((PB, PB), F32), vm((PB, PB), F32), vm((N_GY, 16, 128), F32),
        ],
        flops=1_600_000_000, size=1_000_000, vmem=VMEM_ONE,
    )(
        tile_owner, tile_local, live_count, features, offsets, point_cell.reshape(1, -1),
        w_first.T, b_first.reshape(1, -1), b_second.reshape(1, -1), w_second, w_third, forward_z,
    )


def local(
    features, offsets, point_cell, tile_owner, tile_local, live_count,
    w_first, b_first, w_second, b_second, w_third, w_point, b_point, w_modes,
):
    _, inverse_z, phase_y, back_y, forward_x, back_x = tables(CX * N_GX, CY * N_GY)
    vm = pltpu.VMEM
    modes, sums = stage_one(
        features, offsets, point_cell, tile_owner, tile_local, live_count,
        w_first, b_first, w_second, b_second, w_third,
    )
    modes = lax.all_to_all(modes, "gy", 0, 0, tiled=True)
    mapped = call(
        map_kernel,
        jax.ShapeDtypeStruct((N_GY, BLK * C, NZ), BF16),
        [SM, SM] + [VM] * 2,
        flops=100_000_000, size=1_000_000,
    )(tile_owner, live_count, sums, w_point)
    along_y, slots = call(
        y_kernel,
        (jax.ShapeDtypeStruct((MODES, CX, 128), F32), jax.ShapeDtypeStruct((8, 128), jnp.int32)),
        [VM, VM],
        flops=100_000_000, size=500_000,
    )(modes, phase_y)
    along_y = lax.all_to_all(along_y, "gx", 0, 0, tiled=True)
    lines = call(
        x_kernel,
        jax.ShapeDtypeStruct((N_GX, CX, 128), F32),
        [VM] * 4,
        flops=100_000_000, size=500_000,
    )(along_y, w_modes.reshape(MODES, -1), forward_x, back_x)
    lines = lax.all_to_all(lines, "gx", 0, 0, tiled=True)
    cells = call(
        back_kernel,
        jax.ShapeDtypeStruct((N_GY, 4 * CY + BLK * C, NZ), BF16),
        [VM] * 3,
        flops=100_000_000, size=500_000,
    )(lines, back_y, mapped)
    cells = lax.all_to_all(cells, "gy", 0, 0, tiled=True)
    return call(
        end_kernel,
        jax.ShapeDtypeStruct((CX, CY, C, NZ), F32),
        [SM] + [VM] * 3,
        [vm((N_GY * 4 * CY, 128), F32), vm((CX * CY, C, NZ), F32)],
        flops=100_000_000, size=1_000_000,
    )(slots, cells, inverse_z, b_point.reshape(C, 1))


def solution(mesh):
    both = ("gx", "gy")
    return jax.shard_map(
        local,
        mesh=mesh,
        in_specs=(
            P(None, both), P(None, both), P(both), P(both, None), P(both, None), P(both),
            P(), P(), P(), P(), P(), P(), P(),
            P(None, "gx", "gy", None, None, None),
        ),
        out_specs=P("gx", "gy", None, None),
        check_vma=False,
    )
```

```python
import functools
import math

import jax
import jax.numpy as jnp
import numpy as np
from jax import lax
from jax.experimental import pallas as pl
from jax.experimental.pallas import tpu as pltpu
from jax.sharding import PartitionSpec as P

NZ = 128
CX = 4
CY = 8
SPAN = 16
PB = 128
C = 32
HID = 64
N_GX = 32
N_GY = 16
BLK = 2
LIST = 4
PAIRS = BLK * LIST
MODES = 32
UNROLL = 1
STACK = 32
VMEM_ONE = 62 * 1024 * 1024
F32 = jnp.float32
BF16 = jnp.bfloat16
BEST = lax.Precision.HIGHEST
NN = (((1,), (0,)), ((), ()))
NT = (((1,), (1,)), ((), ()))
TN = (((0,), (0,)), ((), ()))
HALF_PI = (1.5703125, 4.837512969970703125e-4, 7.549789954891882e-8)
SIN_TERMS = (-1.9515295891e-4, 8.3321608736e-3, -1.6666654611e-1)
COS_TERMS = (2.443315711809948e-5, -1.388731625493765e-3, 4.166664568298827e-2)
GELU_A = math.sqrt(2.0 / math.pi)
GELU_B = GELU_A * 0.044715


def iota(shape, dim):
    return lax.broadcasted_iota(jnp.int32, shape, dim)


def dot(a, b, dims=NN):
    return lax.dot_general(a, b, dims, preferred_element_type=F32)


def fine_dot(a, b, dims=NN):
    return lax.dot_general(a, b, dims, precision=BEST, preferred_element_type=F32)


def halves(x):
    high = x.astype(BF16)
    return high, (x - high.astype(F32)).astype(BF16)


def table_dot(table, x):
    high, low = halves(x)
    rows = table.shape[0] // 2
    both = dot(table, high)
    return both[:rows] + both[rows:] + dot(table[:rows], low)


def sin_cos(x):
    count = jnp.floor(x * (2.0 / math.pi) + 0.5)
    rest = x - count * HALF_PI[0]
    rest = rest - count * HALF_PI[1]
    rest = rest - count * HALF_PI[2]
    square = rest * rest
    s = (SIN_TERMS[0] * square + SIN_TERMS[1]) * square + SIN_TERMS[2]
    s = s * square * rest + rest
    c = (COS_TERMS[0] * square + COS_TERMS[1]) * square + COS_TERMS[2]
    c = c * square * square - 0.5 * square + 1.0
    quarter = count.astype(jnp.int32)
    odd = (quarter & 1) != 0
    sine = jnp.where(odd, c, s)
    cosine = jnp.where(odd, s, c)
    sine = jnp.where((quarter & 2) != 0, -sine, sine)
    cosine = jnp.where(((quarter + 1) & 2) != 0, -cosine, cosine)
    return sine, cosine


def angles(length, two_sided):
    orders = np.arange(MODES)
    frequency = np.where(orders < MODES // 2, orders, length - MODES + orders) if two_sided else orders
    turns = np.arange(length)[:, None] * frequency[None, :] % length
    return turns * (2.0 * math.pi / length)


def f32(x):
    return np.ascontiguousarray(x, dtype=np.float32)


def split_table(x):
    high = f32(x).astype(jnp.bfloat16)
    low = (x - high.astype(np.float64)).astype(np.float32).astype(jnp.bfloat16)
    return high, low


def tables(size_x, size_y):
    scale = 1.0 / math.sqrt(size_x * size_y * NZ)
    along_z = angles(NZ, False)
    both = np.stack([np.cos(along_z), -np.sin(along_z)], -1) * scale
    both = both.reshape(NZ, N_GY, 4)
    forward_z = np.concatenate(split_table(both.transpose(2, 1, 0).reshape(4 * N_GY, NZ)), 0)
    inverse_z = np.concatenate(split_table(both.reshape(NZ, 4 * N_GY).T), 1)
    along_y = angles(size_y, True)
    per_row = np.repeat(along_y.T, CX, axis=0)
    phase_y = np.concatenate(split_table(np.cos(per_row)) + split_table(np.sin(per_row)), 0)
    back_y = np.concatenate(split_table(np.concatenate([np.cos(along_y), np.sin(along_y)], 1)), 0)
    along_x = angles(size_x, True)
    forward_x = np.concatenate(split_table(np.concatenate([np.cos(along_x), np.sin(along_x)], 0).T), 0)
    back_x = np.concatenate(split_table(np.concatenate([np.cos(along_x), np.sin(along_x)], 1)), 0)
    return forward_z, inverse_z, phase_y, back_y, forward_x, back_x


def pair_kernel(
    owner, tile, live, feats, offs, cells, w1, b1, b2, w2, w3, fz,
    modes_out, sums,
    cz, sz, w2b, w3b, side, point, feat, sin_p, cos_p, held,
):
    gx = lax.axis_index("gx")
    gy = lax.axis_index("gy")
    pick = ((iota((4 * HID, HID), 0) & (HID - 1)) == iota((4 * HID, HID), 1)).astype(BF16)
    spread = dot(dot(pick, w2[...], NT).astype(BF16), pick, NT)
    same = (iota(spread.shape, 0) // HID) == (iota(spread.shape, 1) // HID)
    w2b[...] = jnp.where(same, spread, 0.0).astype(BF16)
    pick_c = ((iota((4 * C, C), 0) & (C - 1)) == iota((4 * C, C), 1)).astype(BF16)
    spread = dot(dot(pick, w3[...], NT).astype(BF16), pick_c, NT)
    same = (iota(spread.shape, 0) // HID) == (iota(spread.shape, 1) // C)
    w3b[...] = jnp.where(same, 0.5 * spread, 0.0).astype(BF16)
    shape = (HID, 4 * HID)
    pick_t = (iota(shape, 0) == (iota(shape, 1) & (HID - 1))).astype(F32)
    side[0:3, :] = fine_dot(w1[...].astype(F32), pick_t)
    side[3:4, :] = fine_dot(jnp.broadcast_to(b1[...], (8, HID)), pick_t)[0:1]
    side[4:5, :] = fine_dot(jnp.broadcast_to(b2[...], (8, HID)), pick_t)[0:1]
    cell_z = ((iota((NZ // 4, 4 * HID), 1) // HID) * (NZ // 4) + iota((NZ // 4, 4 * HID), 0)).astype(F32)
    sine, cosine = sin_cos(side[2:3, :] * cell_z)
    cz[...] = cosine
    sz[...] = sine
    sums[...] = jnp.zeros_like(sums)
    row_of = iota((PB, PB), 0)
    for b in range(BLK):
        span = slice(b * PB, (b + 1) * PB)
        q = cells[:, span]
        place = [
            ((q // 64) * SPAN).astype(F32) + offs[0:1, span].astype(F32),
            ((q // 8 % 8) * SPAN).astype(F32) + offs[1:2, span].astype(F32),
            ((q % 8) * SPAN).astype(F32) + offs[2:3, span].astype(F32),
        ]
        stack = jnp.where(row_of == 0, place[0], jnp.where(row_of == 1, place[1], place[2]))
        turned = jnp.transpose(stack)
        point[b] = (
            turned[:, 0:1] * side[0:1, :PB] + turned[:, 1:2] * side[1:2, :PB] + turned[:, 2:3] * side[2:3, :PB]
        )
        block = feats[:, span].astype(F32) * (1.0 / math.sqrt(PB))
        feat[b] = jnp.transpose(jnp.concatenate([block] * 4, axis=0))
    for b in range(BLK):

        def one_pair(s, carry, b=b):
            t = tile[b, s]
            x = (CX * gx + t // CY).astype(F32)
            y = (CY * owner[b, s] + t % CY).astype(F32)
            line = side[0:1, :PB] * x + side[1:2, :PB] * y + side[3:4, :PB]
            sine, cosine = sin_cos(line - point[b])
            sin_p[...] = sine
            cos_p[...] = cosine

            def some_cells(i, carry):
                for u in range(UNROLL):
                    g = (i * UNROLL + u) * STACK
                    sp = sin_p[...]
                    cp = cos_p[...]
                    lines = []
                    for k in range(STACK):
                        c = cz[pl.ds(g + k, 1), :]
                        d = sz[pl.ds(g + k, 1), :]
                        lines.append(
                            jnp.concatenate(
                                [sp * c[:, :PB] + cp * d[:, :PB], sp * c[:, PB:] + cp * d[:, PB:]], axis=1
                            ).astype(BF16)
                        )
                    h = dot(jnp.concatenate(lines, axis=0), w2b[...]) + side[4:5, :]
                    th = jnp.tanh(h * (GELU_B * (h * h) + GELU_A))
                    second = (h + h * th).astype(BF16)
                    kern = dot(second, w3b[...])
                    for k in range(STACK):
                        total = jnp.sum(kern[k * PB : (k + 1) * PB] * feat[b], axis=0, keepdims=True)
                        sums[pl.ds((b * LIST + s) * (NZ // 4) + g + k, 1), :] = total
                return carry

            lax.fori_loop(0, NZ // 4 // (UNROLL * STACK), some_cells, 0)
            return carry

        lax.fori_loop(0, live[b], one_pair, 0)
    by_cell = spread_cells(sums[...])
    lane_group = iota((N_GY, 4 * C), 1) // C
    held[...] = jnp.zeros_like(held)
    table = fz[...]
    for j in range(PAIRS):
        both = dot(table, by_cell[0][j])
        full = both[: 4 * N_GY] + both[4 * N_GY :] + dot(table[: 4 * N_GY], by_cell[1][j])
        picked = jnp.zeros((N_GY, 4 * C), F32)
        for g in range(4):
            picked = jnp.where(lane_group == g, full[g * N_GY : (g + 1) * N_GY], picked)
        held[:, j, :] = picked
    lane = iota((1, 128), 1)
    xs = jnp.zeros((1, 128), jnp.int32)
    ys = jnp.zeros((1, 128), jnp.int32)
    on = jnp.zeros((1, 128), jnp.int32)
    for j in range(PAIRS):
        b, s = divmod(j, LIST)
        here = lane == gy * PAIRS + j
        t = tile[b, s]
        xs = jnp.where(here, t // CY, xs)
        ys = jnp.where(here, CY * owner[b, s] + t % CY, ys)
        on = jnp.where(here & (s < live[b]), 1, on)
    for k, v in enumerate((xs, ys, on)):
        held[:, PAIRS + k, :] = jnp.broadcast_to(v.astype(F32), (N_GY, 128))
    modes_out[...] = held[...].astype(modes_out.dtype)


def spread_cells(sums):
    shape = (4 * C, 16 * C)
    copy_c = (
        ((iota(shape, 0) & (C - 1)) == (iota(shape, 1) & (C - 1))) & ((iota(shape, 0) // C) == (iota(shape, 1) // (4 * C)))
    ).astype(BF16)
    terms = []
    for term in halves(sums):
        wide = dot(term, copy_c).astype(BF16)
        terms.append(
            [
                jnp.concatenate([wide[j * 32 : (j + 1) * 32, k * 128 : (k + 1) * 128] for k in range(4)], axis=0)
                for j in range(PAIRS)
            ]
        )
    return terms


def tile_kernel(slots, got, wp, bias, out, raw):
    raw[...] = jnp.zeros_like(raw)
    for n in range(N_GY * BLK):
        v = slots[0, n]

        @pl.when(v >= 0)
        def _(n=n, v=v):
            t = pl.multiple_of((v & (CX * CY - 1)) * (NZ // 4), NZ // 4)
            at = pl.multiple_of((n * LIST + v // (CX * CY)) * (NZ // 4), NZ // 4)
            raw[pl.ds(t, NZ // 4), :] = raw[pl.ds(t, NZ // 4), :] + got[pl.ds(at, NZ // 4), :]

    pick = ((iota((4 * C, C), 0) & (C - 1)) == iota((4 * C, C), 1)).astype(BF16)
    spread = dot(dot(pick, wp[...], NT).astype(BF16), pick, NT)
    same = (iota(spread.shape, 0) // C) == (iota(spread.shape, 1) // C)
    weights = jnp.where(same, spread, 0.0).astype(BF16)
    column = jnp.broadcast_to(bias[...], (C, NZ))
    group = iota((C, NZ), 1) // (NZ // 4)
    for q in range(CX * CY // 4):
        high, low = halves(raw[q * NZ : (q + 1) * NZ, :])
        mapped = dot(weights, high, NT) + dot(weights, low, NT)
        for t in range(4):
            line = jnp.zeros((C, NZ), F32)
            for k in range(4):
                piece = mapped[k * C : (k + 1) * C]
                shift = ((k - t) * (NZ // 4)) % NZ
                line = jnp.where(group == k, piece if shift == 0 else pltpu.roll(piece, shift, 1), line)
            out[q * 4 + t] = line + column


def y_kernel(got, phase, out, slots):
    gy = lax.axis_index("gy")
    full = got[...].astype(F32)
    values = full[:, :PAIRS, :].reshape(N_GY * PAIRS, 128)
    sent = jnp.sum(full[:, PAIRS:, :], axis=0)
    xs, ys, on = sent[0:1], sent[1:2], sent[2:3]
    square = (128, 128)
    hot = ((iota(square, 0).astype(F32) == ys) & (on > 0.5)).astype(BF16)
    turned = dot(phase[...], hot)
    here = (iota((512, 128), 0) & (CX - 1)).astype(F32) == xs
    turned = jnp.where(here, turned, 0.0).astype(BF16)
    both = dot(turned[:256], values.astype(BF16)) + dot(turned[256:], rotated(values, 1.0).astype(BF16))
    result = both[:128] + both[128:]
    out[...] = result.reshape(MODES, CX, 128).astype(out.dtype)
    yi = ys.astype(jnp.int32)
    mine = ((yi // CY) == gy) & (on > 0.5)
    number = xs.astype(jnp.int32) * CY + (yi & (CY - 1)) + (iota((1, 128), 1) & (LIST - 1)) * (CX * CY) + 1
    number = jnp.where(mine, number, 0).astype(BF16)
    group = ((iota(square, 0) // LIST) == iota(square, 1)).astype(BF16)
    slots[...] = dot(jnp.broadcast_to(number, (8, 128)), group).astype(jnp.int32) - 1


def rotated(x, sign):
    up = pltpu.roll(x, 128 - C, 1)
    down = pltpu.roll(x, C, 1)
    real = ((iota(x.shape, 1) // C) & 1) == 0
    return jnp.where(real, sign * up, -sign * down)


def x_kernel(got, weights, forward, back, out):
    size_x = CX * N_GX
    values = got[...].astype(F32).reshape(size_x, 128)
    spectrum = table_dot(forward[...], jnp.concatenate([values, rotated(values, 1.0)], axis=0))
    parts = [spectrum if g == 0 else pltpu.roll(spectrum, 128 - g * C, 1) for g in range(4)]
    high, low = halves(jnp.concatenate(parts, axis=0))
    spread = ((iota((128, C * C), 1) // C) == iota((128, C * C), 0)).astype(BF16)
    wide = dot(high, spread) + dot(low, spread)
    totals = []
    for k in range(2):
        real = wide[(2 * k) * MODES : (2 * k + 1) * MODES]
        imag = wide[(2 * k + 1) * MODES : (2 * k + 2) * MODES]
        sum_r = jnp.zeros((MODES, 128), F32)
        sum_i = jnp.zeros((MODES, 128), F32)
        for j in range(C * C // 128):
            lanes = slice(j * 128, (j + 1) * 128)
            at = (2 * k) * C * C + j * 128
            wr = weights[:, at : at + 128].astype(F32)
            wi = weights[:, at + C * C : at + C * C + 128].astype(F32)
            sum_r = sum_r + real[:, lanes] * wr - imag[:, lanes] * wi
            sum_i = sum_i + real[:, lanes] * wi + imag[:, lanes] * wr
        for v in (sum_r, sum_i):
            v = v + pltpu.roll(v, 64, 1)
            totals.append(v + pltpu.roll(v, 32, 1))
    group = iota((MODES, 128), 1) // C
    r0, i0, r1, i1 = totals
    mixed = jnp.where(group == 0, r0, jnp.where(group == 1, i0, jnp.where(group == 2, r1, i1)))
    other = jnp.where(group == 0, -i0, jnp.where(group == 1, r0, jnp.where(group == 2, -i1, r1)))
    result = table_dot(back[...], jnp.concatenate([mixed, other], axis=0))
    out[...] = result.reshape(N_GX, CX, 128).astype(out.dtype)


def back_kernel(got, back, out):
    lines = [got[:, x, :].astype(F32) for x in range(CX)]
    group = iota((MODES, 128), 1) // C
    turned = []
    for g in range(4):
        line = jnp.zeros((MODES, 128), F32)
        for x in range(CX):
            shift = ((x - g) * C) % 128
            moved = lines[x] if shift == 0 else pltpu.roll(lines[x], shift, 1)
            line = jnp.where(group == x, moved, line)
        turned.append(line)
    r0, i0, r1, i1 = turned
    stack = jnp.concatenate(
        [jnp.concatenate(turned, axis=1), jnp.concatenate([-i0, r0, -i1, r1], axis=1)], axis=0
    )
    result = table_dot(back[...], stack)
    for g in range(4):
        piece = result[:, g * 128 : (g + 1) * 128].reshape(N_GY, CY, 128)
        out[:, g * CY : (g + 1) * CY, :] = piece.astype(out.dtype)


def end_kernel(got, inverse, known, out, wide):
    wide[...] = got[...].astype(F32).reshape(N_GY * 4 * CY, 128)
    for y in range(CY):
        values = wide[pl.ds(y, 4 * N_GY, stride=CY), :].astype(BF16)
        both = dot(values, inverse[...], TN)
        line = both[:, :NZ] + both[:, NZ:]
        for x in range(CX):
            h = line[x * C : (x + 1) * C] + known[x * CY + y]
            th = jnp.tanh(h * (GELU_B * (h * h) + GELU_A))
            out[x, y] = 0.5 * (h + h * th)


def call(kernel, out_shape, in_specs, scratch=(), flops=0, size=0, vmem=40 * 1024 * 1024):
    return pl.pallas_call(
        kernel,
        out_shape=out_shape,
        in_specs=in_specs,
        scratch_shapes=list(scratch),
        compiler_params=pltpu.CompilerParams(vmem_limit_bytes=vmem),
        cost_estimate=pl.CostEstimate(flops=flops, bytes_accessed=size, transcendentals=0),
    )


VM = pl.BlockSpec(memory_space=pltpu.VMEM)
SM = pl.BlockSpec(memory_space=pltpu.SMEM)


def stage_one(
    features, offsets, point_cell, tile_owner, tile_local, live_count,
    w_first, b_first, w_second, b_second, w_third, *_,
):
    forward_z = tables(CX * N_GX, CY * N_GY)[0]
    vm = pltpu.VMEM
    return call(
        pair_kernel,
        (
            jax.ShapeDtypeStruct((N_GY, 16, 128), BF16),
            jax.ShapeDtypeStruct((PAIRS * NZ // 4, 4 * C), F32),
        ),
        [SM, SM, SM] + [VM] * 9,
        [
            vm((NZ // 4, 4 * HID), F32), vm((NZ // 4, 4 * HID), F32),
            vm((4 * HID, 4 * HID), BF16), vm((4 * HID, 4 * C), BF16),
            vm((8, 4 * HID), F32), vm((BLK, PB, PB), F32), vm((BLK, PB, PB), F32),
            vm((PB, PB), F32), vm((PB, PB), F32), vm((N_GY, 16, 128), F32),
        ],
        flops=1_600_000_000, size=1_000_000, vmem=VMEM_ONE,
    )(
        tile_owner, tile_local, live_count, features, offsets, point_cell.reshape(1, -1),
        w_first.T, b_first.reshape(1, -1), b_second.reshape(1, -1), w_second, w_third, forward_z,
    )


def local(
    features, offsets, point_cell, tile_owner, tile_local, live_count,
    w_first, b_first, w_second, b_second, w_third, w_point, b_point, w_modes,
):
    _, inverse_z, phase_y, back_y, forward_x, back_x = tables(CX * N_GX, CY * N_GY)
    vm = pltpu.VMEM
    modes, sums = stage_one(
        features, offsets, point_cell, tile_owner, tile_local, live_count,
        w_first, b_first, w_second, b_second, w_third,
    )
    modes = lax.all_to_all(modes, "gy", 0, 0, tiled=True)
    sums = lax.all_gather(sums, "gy", axis=0, tiled=True)
    along_y, slots = call(
        y_kernel,
        (jax.ShapeDtypeStruct((MODES, CX, 128), F32), jax.ShapeDtypeStruct((8, 128), jnp.int32)),
        [VM, VM],
        flops=100_000_000, size=500_000,
    )(modes, phase_y)
    along_y = lax.all_to_all(along_y, "gx", 0, 0, tiled=True)
    lines = call(
        x_kernel,
        jax.ShapeDtypeStruct((N_GX, CX, 128), F32),
        [VM] * 4,
        flops=100_000_000, size=500_000,
    )(along_y, w_modes.reshape(MODES, -1), forward_x, back_x)
    lines = lax.all_to_all(lines, "gx", 0, 0, tiled=True)
    cells = call(
        back_kernel,
        jax.ShapeDtypeStruct((N_GY, 4 * CY, 128), BF16),
        [VM] * 2,
        flops=100_000_000, size=500_000,
    )(lines, back_y)
    known = call(
        tile_kernel,
        jax.ShapeDtypeStruct((CX * CY, C, NZ), F32),
        [SM] + [VM] * 3,
        [vm((CX * CY * NZ // 4, 4 * C), F32)],
        flops=100_000_000, size=2_500_000,
    )(slots, sums, w_point, b_point.reshape(C, 1))
    cells = lax.all_to_all(cells, "gy", 0, 0, tiled=True)
    return call(
        end_kernel,
        jax.ShapeDtypeStruct((CX, CY, C, NZ), F32),
        [VM] * 3,
        [vm((N_GY * 4 * CY, 128), F32)],
        flops=100_000_000, size=1_000_000,
    )(cells, inverse_z, known)


def solution(mesh):
    both = ("gx", "gy")
    return jax.shard_map(
        local,
        mesh=mesh,
        in_specs=(
            P(None, both), P(None, both), P(both), P(both, None), P(both, None), P(both),
            P(), P(), P(), P(), P(), P(), P(),
            P(None, "gx", "gy", None, None, None),
        ),
        out_specs=P("gx", "gy", None, None),
        check_vma=False,
    )
```

```python
import functools
import math

import jax
import jax.numpy as jnp
import numpy as np
from jax import lax
from jax.experimental import pallas as pl
from jax.experimental.pallas import tpu as pltpu
from jax.sharding import PartitionSpec as P

NZ = 128
CX = 4
CY = 8
SPAN = 16
PB = 128
C = 32
HID = 64
N_GX = 32
N_GY = 16
BLK = 2
LIST = 4
PAIRS = BLK * LIST
MODES = 32
ANCHOR = 16
VMEM_ONE = 62 * 1024 * 1024
F32 = jnp.float32
BF16 = jnp.bfloat16
BEST = lax.Precision.HIGHEST
NN = (((1,), (0,)), ((), ()))
NT = (((1,), (1,)), ((), ()))
TN = (((0,), (0,)), ((), ()))
HALF_PI = (1.5703125, 4.837512969970703125e-4, 7.549789954891882e-8)
SIN_TERMS = (-1.9515295891e-4, 8.3321608736e-3, -1.6666654611e-1)
COS_TERMS = (2.443315711809948e-5, -1.388731625493765e-3, 4.166664568298827e-2)
GELU_A = math.sqrt(2.0 / math.pi)
GELU_B = GELU_A * 0.044715


def iota(shape, dim):
    return lax.broadcasted_iota(jnp.int32, shape, dim)


def dot(a, b, dims=NN):
    return lax.dot_general(a, b, dims, preferred_element_type=F32)


def fine_dot(a, b, dims=NN):
    return lax.dot_general(a, b, dims, precision=BEST, preferred_element_type=F32)


def halves(x):
    high = x.astype(BF16)
    return high, (x - high.astype(F32)).astype(BF16)


def table_dot(table, x):
    high, low = halves(x)
    rows = table.shape[0] // 2
    both = dot(table, high)
    return both[:rows] + both[rows:] + dot(table[:rows], low)


def sin_cos(x):
    count = jnp.floor(x * (2.0 / math.pi) + 0.5)
    rest = x - count * HALF_PI[0]
    rest = rest - count * HALF_PI[1]
    rest = rest - count * HALF_PI[2]
    square = rest * rest
    s = (SIN_TERMS[0] * square + SIN_TERMS[1]) * square + SIN_TERMS[2]
    s = s * square * rest + rest
    c = (COS_TERMS[0] * square + COS_TERMS[1]) * square + COS_TERMS[2]
    c = c * square * square - 0.5 * square + 1.0
    quarter = count.astype(jnp.int32)
    odd = (quarter & 1) != 0
    sine = jnp.where(odd, c, s)
    cosine = jnp.where(odd, s, c)
    sine = jnp.where((quarter & 2) != 0, -sine, sine)
    cosine = jnp.where(((quarter + 1) & 2) != 0, -cosine, cosine)
    return sine, cosine


def angles(length, two_sided):
    orders = np.arange(MODES)
    frequency = np.where(orders < MODES // 2, orders, length - MODES + orders) if two_sided else orders
    turns = np.arange(length)[:, None] * frequency[None, :] % length
    return turns * (2.0 * math.pi / length)


def f32(x):
    return np.ascontiguousarray(x, dtype=np.float32)


def split_table(x):
    high = f32(x).astype(jnp.bfloat16)
    low = (x - high.astype(np.float64)).astype(np.float32).astype(jnp.bfloat16)
    return high, low


def tables(size_x, size_y):
    scale = 1.0 / math.sqrt(size_x * size_y * NZ)
    along_z = angles(NZ, False)
    both = np.stack([np.cos(along_z), -np.sin(along_z)], -1) * scale
    both = both.reshape(NZ, N_GY, 4)
    forward_z = np.concatenate(split_table(both.transpose(2, 1, 0).reshape(4 * N_GY, NZ)), 0)
    inverse_z = np.concatenate(split_table(both.reshape(NZ, 4 * N_GY).T), 1)
    along_y = angles(size_y, True)
    per_row = np.repeat(along_y.T, CX, axis=0)
    phase_y = np.concatenate(split_table(np.cos(per_row)) + split_table(np.sin(per_row)), 0)
    back_y = np.concatenate(split_table(np.concatenate([np.cos(along_y), np.sin(along_y)], 1)), 0)
    along_x = angles(size_x, True)
    forward_x = np.concatenate(split_table(np.concatenate([np.cos(along_x), np.sin(along_x)], 0).T), 0)
    back_x = np.concatenate(split_table(np.concatenate([np.cos(along_x), np.sin(along_x)], 1)), 0)
    return forward_z, inverse_z, phase_y, back_y, forward_x, back_x


def pair_kernel(
    owner, tile, live, feats, offs, cells, w1, b1, b2, w2, w3, fz,
    sent,
    sums, cz, sz, w2b, w3b, side, point, feat, sin_p, cos_p, held,
):
    gx = lax.axis_index("gx")
    gy = lax.axis_index("gy")
    pick = ((iota((4 * HID, HID), 0) & (HID - 1)) == iota((4 * HID, HID), 1)).astype(BF16)
    spread = dot(dot(pick, w2[...], NT).astype(BF16), pick, NT)
    same = (iota(spread.shape, 0) // HID) == (iota(spread.shape, 1) // HID)
    w2b[...] = jnp.where(same, spread, 0.0)
    pick_c = ((iota((4 * C, C), 0) & (C - 1)) == iota((4 * C, C), 1)).astype(BF16)
    spread = dot(dot(pick, w3[...], NT).astype(BF16), pick_c, NT)
    same = (iota(spread.shape, 0) // HID) == (iota(spread.shape, 1) // C)
    w3b[...] = jnp.where(same, 0.5 * spread, 0.0)
    shape = (HID, 4 * HID)
    pick_t = (iota(shape, 0) == (iota(shape, 1) & (HID - 1))).astype(F32)
    side[0:3, :] = fine_dot(w1[...].astype(F32), pick_t)
    side[3:4, :] = fine_dot(jnp.broadcast_to(b1[...], (8, HID)), pick_t)[0:1]
    side[4:5, :] = fine_dot(jnp.broadcast_to(b2[...], (8, HID)), pick_t)[0:1]
    cell_z = ((iota((NZ // 4, 4 * HID), 1) // HID) * (NZ // 4) + iota((NZ // 4, 4 * HID), 0)).astype(F32)
    sine, cosine = sin_cos(side[2:3, :] * cell_z)
    cz[...] = cosine
    sz[...] = sine
    side[5:6, :] = 2.0 * sin_cos(jnp.broadcast_to(side[2:3, :], (8, 4 * HID)))[1][0:1]
    sums[...] = jnp.zeros_like(sums)
    row_of = iota((PB, PB), 0)
    for b in range(BLK):
        span = slice(b * PB, (b + 1) * PB)
        q = cells[:, span]
        place = [
            ((q // 64) * SPAN).astype(F32) + offs[0:1, span].astype(F32),
            ((q // 8 % 8) * SPAN).astype(F32) + offs[1:2, span].astype(F32),
            ((q % 8) * SPAN).astype(F32) + offs[2:3, span].astype(F32),
        ]
        stack = jnp.where(row_of == 0, place[0], jnp.where(row_of == 1, place[1], place[2]))
        turned = jnp.transpose(stack)
        point[b] = (
            turned[:, 0:1] * side[0:1, :PB] + turned[:, 1:2] * side[1:2, :PB] + turned[:, 2:3] * side[2:3, :PB]
        )
        block = feats[:, span].astype(F32) * (1.0 / math.sqrt(PB))
        feat[b] = jnp.transpose(jnp.concatenate([block] * 4, axis=0))
    for b in range(BLK):

        def one_pair(s, carry, b=b):
            t = tile[b, s]
            x = (CX * gx + t // CY).astype(F32)
            y = (CY * owner[b, s] + t % CY).astype(F32)
            line = side[0:1, :PB] * x + side[1:2, :PB] * y + side[3:4, :PB]
            sine, cosine = sin_cos(line - point[b])
            sin_p[...] = sine
            cos_p[...] = cosine
            twice = side[5:6, :PB]

            lines = []
            for g in range(NZ // 4):
                if g % ANCHOR < 2:
                    sp = sin_p[...]
                    cp = cos_p[...]
                    c = cz[g : g + 1, :]
                    d = sz[g : g + 1, :]
                    now = sp * c[:, :PB] + cp * d[:, :PB], sp * c[:, PB:] + cp * d[:, PB:]
                else:
                    now = twice * last[0] - before[0], twice * last[1] - before[1]
                if g % ANCHOR:
                    before = last
                last = now
                lines.append(jnp.concatenate(now, axis=1))
            h = dot(jnp.concatenate(lines, axis=0), w2b[...]) + side[4:5, :]
            th = jnp.tanh(h * (GELU_B * (h * h) + GELU_A))
            kern = dot(h + h * th, w3b[...])
            for g in range(NZ // 4):
                total = jnp.sum(kern[g * PB : (g + 1) * PB] * feat[b], axis=0, keepdims=True)
                sums[pl.ds((b * LIST + s) * (NZ // 4) + g, 1), :] = total
            return carry

        lax.fori_loop(0, live[b], one_pair, 0)
    by_cell = spread_cells(sums[...])
    lane_group = iota((N_GY, 4 * C), 1) // C
    held[...] = jnp.zeros_like(held)
    table = fz[...]
    for j in range(PAIRS):
        both = dot(table, by_cell[0][j])
        full = both[: 4 * N_GY] + both[4 * N_GY :] + dot(table[: 4 * N_GY], by_cell[1][j])
        picked = jnp.zeros((N_GY, 4 * C), F32)
        for g in range(4):
            picked = jnp.where(lane_group == g, full[g * N_GY : (g + 1) * N_GY], picked)
        held[:, j, :] = picked
    lane = iota((1, 128), 1)
    xs = jnp.zeros((1, 128), jnp.int32)
    ys = jnp.zeros((1, 128), jnp.int32)
    on = jnp.zeros((1, 128), jnp.int32)
    for j in range(PAIRS):
        b, s = divmod(j, LIST)
        here = lane == gy * PAIRS + j
        t = tile[b, s]
        xs = jnp.where(here, t // CY, xs)
        ys = jnp.where(here, CY * owner[b, s] + t % CY, ys)
        on = jnp.where(here & (s < live[b]), 1, on)
    for k, v in enumerate((xs, ys, on)):
        held[:, PAIRS + k, :] = jnp.broadcast_to(v.astype(F32), (N_GY, 128))
    sent[:, :16, :] = held[...].astype(sent.dtype)
    sent[:, 16:, :] = jnp.zeros((N_GY, BLK * NZ // 4, 4 * C), sent.dtype)
    for j in range(PAIRS):
        b, s = divmod(j, LIST)

        @pl.when(s < live[b])
        def _(b=b, s=s, j=j):
            at = 16 + b * (NZ // 4)
            rows = sums[j * (NZ // 4) : (j + 1) * (NZ // 4), :]
            sent[owner[b, s], at : at + NZ // 4, :] = rows.astype(sent.dtype)


def spread_cells(sums):
    shape = (4 * C, 16 * C)
    copy_c = (
        ((iota(shape, 0) & (C - 1)) == (iota(shape, 1) & (C - 1))) & ((iota(shape, 0) // C) == (iota(shape, 1) // (4 * C)))
    ).astype(BF16)
    terms = []
    for term in halves(sums):
        wide = dot(term, copy_c).astype(BF16)
        terms.append(
            [
                jnp.concatenate([wide[j * 32 : (j + 1) * 32, k * 128 : (k + 1) * 128] for k in range(4)], axis=0)
                for j in range(PAIRS)
            ]
        )
    return terms


def tile_kernel(slots, got, wp, bias, out, raw):
    raw[...] = jnp.zeros_like(raw)
    for n in range(N_GY * BLK):
        src, b = divmod(n, BLK)
        v = slots[0, n]

        @pl.when(v >= 0)
        def _(src=src, b=b, v=v):
            t = pl.multiple_of(v * (NZ // 4), NZ // 4)
            at = 16 + b * (NZ // 4)
            raw[pl.ds(t, NZ // 4), :] = raw[pl.ds(t, NZ // 4), :] + got[src, at : at + NZ // 4, :].astype(F32)

    pick = ((iota((4 * C, C), 0) & (C - 1)) == iota((4 * C, C), 1)).astype(BF16)
    spread = dot(dot(pick, wp[...], NT).astype(BF16), pick, NT)
    same = (iota(spread.shape, 0) // C) == (iota(spread.shape, 1) // C)
    weights = jnp.where(same, spread, 0.0).astype(BF16)
    column = jnp.broadcast_to(bias[...], (C, NZ))
    group = iota((C, NZ), 1) // (NZ // 4)
    for q in range(CX * CY // 4):
        high, low = halves(raw[q * NZ : (q + 1) * NZ, :])
        mapped = dot(weights, high, NT) + dot(weights, low, NT)
        for t in range(4):
            line = jnp.zeros((C, NZ), F32)
            for k in range(4):
                piece = mapped[k * C : (k + 1) * C]
                shift = ((k - t) * (NZ // 4)) % NZ
                line = jnp.where(group == k, piece if shift == 0 else pltpu.roll(piece, shift, 1), line)
            out[q * 4 + t] = line + column


def y_kernel(got, phase, out, slots):
    gy = lax.axis_index("gy")
    full = got[:, :16, :].astype(F32)
    values = full[:, :PAIRS, :].reshape(N_GY * PAIRS, 128)
    sent = jnp.sum(full[:, PAIRS:, :], axis=0)
    xs, ys, on = sent[0:1], sent[1:2], sent[2:3]
    square = (128, 128)
    hot = ((iota(square, 0).astype(F32) == ys) & (on > 0.5)).astype(BF16)
    turned = dot(phase[...], hot)
    here = (iota((512, 128), 0) & (CX - 1)).astype(F32) == xs
    turned = jnp.where(here, turned, 0.0).astype(BF16)
    both = dot(turned[:256], values.astype(BF16)) + dot(turned[256:], rotated(values, 1.0).astype(BF16))
    result = both[:128] + both[128:]
    out[...] = result.reshape(MODES, CX, 128).astype(out.dtype)
    yi = ys.astype(jnp.int32)
    mine = ((yi // CY) == gy) & (on > 0.5)
    number = jnp.where(mine, xs.astype(jnp.int32) * CY + (yi & (CY - 1)) + 1, 0).astype(BF16)
    group = ((iota(square, 0) // LIST) == iota(square, 1)).astype(BF16)
    slots[...] = dot(jnp.broadcast_to(number, (8, 128)), group).astype(jnp.int32) - 1


def rotated(x, sign):
    up = pltpu.roll(x, 128 - C, 1)
    down = pltpu.roll(x, C, 1)
    real = ((iota(x.shape, 1) // C) & 1) == 0
    return jnp.where(real, sign * up, -sign * down)


def x_kernel(got, weights, forward, back, out):
    size_x = CX * N_GX
    values = got[...].astype(F32).reshape(size_x, 128)
    spectrum = table_dot(forward[...], jnp.concatenate([values, rotated(values, 1.0)], axis=0))
    parts = [spectrum if g == 0 else pltpu.roll(spectrum, 128 - g * C, 1) for g in range(4)]
    high, low = halves(jnp.concatenate(parts, axis=0))
    spread = ((iota((128, C * C), 1) // C) == iota((128, C * C), 0)).astype(BF16)
    wide = dot(high, spread) + dot(low, spread)
    totals = []
    for k in range(2):
        real = wide[(2 * k) * MODES : (2 * k + 1) * MODES]
        imag = wide[(2 * k + 1) * MODES : (2 * k + 2) * MODES]
        sum_r = jnp.zeros((MODES, 128), F32)
        sum_i = jnp.zeros((MODES, 128), F32)
        for j in range(C * C // 128):
            lanes = slice(j * 128, (j + 1) * 128)
            at = (2 * k) * C * C + j * 128
            wr = weights[:, at : at + 128].astype(F32)
            wi = weights[:, at + C * C : at + C * C + 128].astype(F32)
            sum_r = sum_r + real[:, lanes] * wr - imag[:, lanes] * wi
            sum_i = sum_i + real[:, lanes] * wi + imag[:, lanes] * wr
        for v in (sum_r, sum_i):
            v = v + pltpu.roll(v, 64, 1)
            totals.append(v + pltpu.roll(v, 32, 1))
    group = iota((MODES, 128), 1) // C
    r0, i0, r1, i1 = totals
    mixed = jnp.where(group == 0, r0, jnp.where(group == 1, i0, jnp.where(group == 2, r1, i1)))
    other = jnp.where(group == 0, -i0, jnp.where(group == 1, r0, jnp.where(group == 2, -i1, r1)))
    result = table_dot(back[...], jnp.concatenate([mixed, other], axis=0))
    out[...] = result.reshape(N_GX, CX, 128).astype(out.dtype)


def back_kernel(got, back, out):
    lines = [got[:, x, :].astype(F32) for x in range(CX)]
    group = iota((MODES, 128), 1) // C
    turned = []
    for g in range(4):
        line = jnp.zeros((MODES, 128), F32)
        for x in range(CX):
            shift = ((x - g) * C) % 128
            moved = lines[x] if shift == 0 else pltpu.roll(lines[x], shift, 1)
            line = jnp.where(group == x, moved, line)
        turned.append(line)
    r0, i0, r1, i1 = turned
    stack = jnp.concatenate(
        [jnp.concatenate(turned, axis=1), jnp.concatenate([-i0, r0, -i1, r1], axis=1)], axis=0
    )
    result = table_dot(back[...], stack)
    for g in range(4):
        piece = result[:, g * 128 : (g + 1) * 128].reshape(N_GY, CY, 128)
        out[:, g * CY : (g + 1) * CY, :] = piece.astype(out.dtype)


def end_kernel(got, inverse, known, out, wide):
    wide[...] = got[...].astype(F32).reshape(N_GY * 4 * CY, 128)
    for y in range(CY):
        values = wide[pl.ds(y, 4 * N_GY, stride=CY), :].astype(BF16)
        both = dot(values, inverse[...], TN)
        line = both[:, :NZ] + both[:, NZ:]
        for x in range(CX):
            h = line[x * C : (x + 1) * C] + known[x * CY + y]
            th = jnp.tanh(h * (GELU_B * (h * h) + GELU_A))
            out[x, y] = 0.5 * (h + h * th)


def call(kernel, out_shape, in_specs, scratch=(), flops=0, size=0, vmem=40 * 1024 * 1024):
    return pl.pallas_call(
        kernel,
        out_shape=out_shape,
        in_specs=in_specs,
        scratch_shapes=list(scratch),
        compiler_params=pltpu.CompilerParams(vmem_limit_bytes=vmem),
        cost_estimate=pl.CostEstimate(flops=flops, bytes_accessed=size, transcendentals=0),
    )


VM = pl.BlockSpec(memory_space=pltpu.VMEM)
SM = pl.BlockSpec(memory_space=pltpu.SMEM)


def stage_one(
    features, offsets, point_cell, tile_owner, tile_local, live_count,
    w_first, b_first, w_second, b_second, w_third, *_,
):
    forward_z = tables(CX * N_GX, CY * N_GY)[0]
    vm = pltpu.VMEM
    return call(
        pair_kernel,
        jax.ShapeDtypeStruct((N_GY, 16 + BLK * NZ // 4, 128), BF16),
        [SM, SM, SM] + [VM] * 9,
        [
            vm((PAIRS * NZ // 4, 4 * C), F32),
            vm((NZ // 4, 4 * HID), F32), vm((NZ // 4, 4 * HID), F32),
            vm((4 * HID, 4 * HID), F32), vm((4 * HID, 4 * C), F32),
            vm((8, 4 * HID), F32), vm((BLK, PB, PB), F32), vm((BLK, PB, PB), F32),
            vm((PB, PB), F32), vm((PB, PB), F32), vm((N_GY, 16, 128), F32),
        ],
        flops=1_600_000_000, size=1_000_000, vmem=VMEM_ONE,
    )(
        tile_owner, tile_local, live_count, features, offsets, point_cell.reshape(1, -1),
        w_first.T, b_first.reshape(1, -1), b_second.reshape(1, -1), w_second, w_third, forward_z,
    )


def local(
    features, offsets, point_cell, tile_owner, tile_local, live_count,
    w_first, b_first, w_second, b_second, w_third, w_point, b_point, w_modes,
):
    _, inverse_z, phase_y, back_y, forward_x, back_x = tables(CX * N_GX, CY * N_GY)
    vm = pltpu.VMEM
    sent = stage_one(
        features, offsets, point_cell, tile_owner, tile_local, live_count,
        w_first, b_first, w_second, b_second, w_third,
    )
    sent = lax.all_to_all(sent, "gy", 0, 0, tiled=True)
    along_y, slots = call(
        y_kernel,
        (jax.ShapeDtypeStruct((MODES, CX, 128), F32), jax.ShapeDtypeStruct((8, 128), jnp.int32)),
        [VM, VM],
        flops=100_000_000, size=500_000,
    )(sent, phase_y)
    along_y = lax.all_to_all(along_y, "gx", 0, 0, tiled=True)
    lines = call(
        x_kernel,
        jax.ShapeDtypeStruct((N_GX, CX, 128), F32),
        [VM] * 4,
        flops=100_000_000, size=500_000,
    )(along_y, w_modes.reshape(MODES, -1), forward_x, back_x)
    lines = lax.all_to_all(lines, "gx", 0, 0, tiled=True)
    cells = call(
        back_kernel,
        jax.ShapeDtypeStruct((N_GY, 4 * CY, 128), BF16),
        [VM] * 2,
        flops=100_000_000, size=500_000,
    )(lines, back_y)
    known = call(
        tile_kernel,
        jax.ShapeDtypeStruct((CX * CY, C, NZ), F32),
        [SM] + [VM] * 3,
        [vm((CX * CY * NZ // 4, 4 * C), F32)],
        flops=100_000_000, size=2_500_000,
    )(slots, sent, w_point, b_point.reshape(C, 1))
    cells = lax.all_to_all(cells, "gy", 0, 0, tiled=True)
    return call(
        end_kernel,
        jax.ShapeDtypeStruct((CX, CY, C, NZ), F32),
        [VM] * 3,
        [vm((N_GY * 4 * CY, 128), F32)],
        flops=100_000_000, size=1_000_000,
    )(cells, inverse_z, known)


def solution(mesh):
    both = ("gx", "gy")
    return jax.shard_map(
        local,
        mesh=mesh,
        in_specs=(
            P(None, both), P(None, both), P(both), P(both, None), P(both, None), P(both),
            P(), P(), P(), P(), P(), P(), P(),
            P(None, "gx", "gy", None, None, None),
        ),
        out_specs=P("gx", "gy", None, None),
        check_vma=False,
    )
```

```python
import functools
import math

import jax
import jax.numpy as jnp
import numpy as np
from jax import lax
from jax.experimental import pallas as pl
from jax.experimental.pallas import tpu as pltpu
from jax.sharding import PartitionSpec as P

NZ = 128
CX = 4
CY = 8
SPAN = 16
PB = 128
C = 32
HID = 64
N_GX = 32
N_GY = 16
BLK = 2
LIST = 4
PAIRS = BLK * LIST
MODES = 32
ANCHOR = 16
VMEM_ONE = 62 * 1024 * 1024
F32 = jnp.float32
BF16 = jnp.bfloat16
BEST = lax.Precision.HIGHEST
NN = (((1,), (0,)), ((), ()))
NT = (((1,), (1,)), ((), ()))
TN = (((0,), (0,)), ((), ()))
HALF_PI = (1.5703125, 4.837512969970703125e-4, 7.549789954891882e-8)
SIN_TERMS = (-1.9515295891e-4, 8.3321608736e-3, -1.6666654611e-1)
COS_TERMS = (2.443315711809948e-5, -1.388731625493765e-3, 4.166664568298827e-2)
GELU_A = math.sqrt(2.0 / math.pi)
GELU_B = GELU_A * 0.044715


def iota(shape, dim):
    return lax.broadcasted_iota(jnp.int32, shape, dim)


def dot(a, b, dims=NN):
    return lax.dot_general(a, b, dims, preferred_element_type=F32)


def fine_dot(a, b, dims=NN):
    return lax.dot_general(a, b, dims, precision=BEST, preferred_element_type=F32)


def halves(x):
    high = x.astype(BF16)
    return high, (x - high.astype(F32)).astype(BF16)


def table_dot(table, x):
    high, low = halves(x)
    rows = table.shape[0] // 2
    both = dot(table, high)
    return both[:rows] + both[rows:] + dot(table[:rows], low)


def sin_cos(x):
    count = jnp.floor(x * (2.0 / math.pi) + 0.5)
    rest = x - count * HALF_PI[0]
    rest = rest - count * HALF_PI[1]
    rest = rest - count * HALF_PI[2]
    square = rest * rest
    s = (SIN_TERMS[0] * square + SIN_TERMS[1]) * square + SIN_TERMS[2]
    s = s * square * rest + rest
    c = (COS_TERMS[0] * square + COS_TERMS[1]) * square + COS_TERMS[2]
    c = c * square * square - 0.5 * square + 1.0
    quarter = count.astype(jnp.int32)
    odd = (quarter & 1) != 0
    sine = jnp.where(odd, c, s)
    cosine = jnp.where(odd, s, c)
    sine = jnp.where((quarter & 2) != 0, -sine, sine)
    cosine = jnp.where(((quarter + 1) & 2) != 0, -cosine, cosine)
    return sine, cosine


def angles(length, two_sided):
    orders = np.arange(MODES)
    frequency = np.where(orders < MODES // 2, orders, length - MODES + orders) if two_sided else orders
    turns = np.arange(length)[:, None] * frequency[None, :] % length
    return turns * (2.0 * math.pi / length)


def f32(x):
    return np.ascontiguousarray(x, dtype=np.float32)


def split_table(x):
    high = f32(x).astype(jnp.bfloat16)
    low = (x - high.astype(np.float64)).astype(np.float32).astype(jnp.bfloat16)
    return high, low


def tables(size_x, size_y):
    scale = 1.0 / math.sqrt(size_x * size_y * NZ)
    along_z = angles(NZ, False)
    both = np.stack([np.cos(along_z), -np.sin(along_z)], -1) * scale
    both = both.reshape(NZ, N_GY, 4)
    forward_z = np.concatenate(split_table(both.transpose(2, 1, 0).reshape(4 * N_GY, NZ)), 0)
    inverse_z = np.concatenate(split_table(both.reshape(NZ, 4 * N_GY).T), 1)
    along_y = angles(size_y, True)
    per_row = np.repeat(along_y.T, CX, axis=0)
    phase_y = np.concatenate(split_table(np.cos(per_row)) + split_table(np.sin(per_row)), 0)
    back_y = np.concatenate(split_table(np.concatenate([np.cos(along_y), np.sin(along_y)], 1)), 0)
    along_x = angles(size_x, True)
    forward_x = np.concatenate(split_table(np.concatenate([np.cos(along_x), np.sin(along_x)], 0).T), 0)
    back_x = np.concatenate(split_table(np.concatenate([np.cos(along_x), np.sin(along_x)], 1)), 0)
    return forward_z, inverse_z, phase_y, back_y, forward_x, back_x


def pair_kernel(
    owner, tile, live, feats, offs, cells, w1, b1, b2, w2, w3, fz,
    sent,
    sums, cz, sz, w2b, w3b, side, point, feat, sin_p, cos_p, held,
):
    gx = lax.axis_index("gx")
    gy = lax.axis_index("gy")
    pick = ((iota((4 * HID, HID), 0) & (HID - 1)) == iota((4 * HID, HID), 1)).astype(BF16)
    spread = dot(dot(pick, w2[...], NT).astype(BF16), pick, NT)
    same = (iota(spread.shape, 0) // HID) == (iota(spread.shape, 1) // HID)
    w2b[...] = jnp.where(same, spread, 0.0)
    pick_c = ((iota((4 * C, C), 0) & (C - 1)) == iota((4 * C, C), 1)).astype(BF16)
    spread = dot(dot(pick, w3[...], NT).astype(BF16), pick_c, NT)
    same = (iota(spread.shape, 0) // HID) == (iota(spread.shape, 1) // C)
    w3b[...] = jnp.where(same, 0.5 * spread, 0.0)
    shape = (HID, 4 * HID)
    pick_t = (iota(shape, 0) == (iota(shape, 1) & (HID - 1))).astype(F32)
    side[0:3, :] = fine_dot(w1[...].astype(F32), pick_t)
    side[3:4, :] = fine_dot(jnp.broadcast_to(b1[...], (8, HID)), pick_t)[0:1]
    side[4:5, :] = fine_dot(jnp.broadcast_to(b2[...], (8, HID)), pick_t)[0:1]
    cell_z = ((iota((NZ // 4, 4 * HID), 1) // HID) * (NZ // 4) + iota((NZ // 4, 4 * HID), 0)).astype(F32)
    sine, cosine = sin_cos(side[2:3, :] * cell_z)
    cz[...] = cosine
    sz[...] = sine
    side[5:6, :] = 2.0 * sin_cos(jnp.broadcast_to(side[2:3, :], (8, 4 * HID)))[1][0:1]
    sums[...] = jnp.zeros_like(sums)
    row_of = iota((PB, PB), 0)
    for b in range(BLK):
        span = slice(b * PB, (b + 1) * PB)
        q = cells[:, span]
        place = [
            ((q // 64) * SPAN).astype(F32) + offs[0:1, span].astype(F32),
            ((q // 8 % 8) * SPAN).astype(F32) + offs[1:2, span].astype(F32),
            ((q % 8) * SPAN).astype(F32) + offs[2:3, span].astype(F32),
        ]
        stack = jnp.where(row_of == 0, place[0], jnp.where(row_of == 1, place[1], place[2]))
        turned = jnp.transpose(stack)
        point[b] = (
            turned[:, 0:1] * side[0:1, :PB] + turned[:, 1:2] * side[1:2, :PB] + turned[:, 2:3] * side[2:3, :PB]
        )
        block = feats[:, span].astype(F32) * (1.0 / math.sqrt(PB))
        feat[b] = jnp.transpose(jnp.concatenate([block] * 4, axis=0))
    for b in range(BLK):

        def one_pair(s, carry, b=b):
            t = tile[b, s]
            x = (CX * gx + t // CY).astype(F32)
            y = (CY * owner[b, s] + t % CY).astype(F32)
            line = side[0:1, :PB] * x + side[1:2, :PB] * y + side[3:4, :PB]
            sine, cosine = sin_cos(line - point[b])
            sin_p[...] = sine
            cos_p[...] = cosine
            twice = side[5:6, :PB]

            lines = []
            for g in range(NZ // 4):
                if g % ANCHOR < 2:
                    sp = sin_p[...]
                    cp = cos_p[...]
                    c = cz[g : g + 1, :]
                    d = sz[g : g + 1, :]
                    now = sp * c[:, :PB] + cp * d[:, :PB], sp * c[:, PB:] + cp * d[:, PB:]
                else:
                    now = twice * last[0] - before[0], twice * last[1] - before[1]
                if g % ANCHOR:
                    before = last
                last = now
                lines.append(jnp.concatenate(now, axis=1))
            h = dot(jnp.concatenate(lines, axis=0), w2b[...]) + side[4:5, :]
            th = jnp.tanh(h * (GELU_B * (h * h) + GELU_A))
            kern = dot(h + h * th, w3b[...])
            for g in range(NZ // 4):
                total = jnp.sum(kern[g * PB : (g + 1) * PB] * feat[b], axis=0, keepdims=True)
                sums[pl.ds((b * LIST + s) * (NZ // 4) + g, 1), :] = total
            return carry

        lax.fori_loop(0, live[b], one_pair, 0)
    by_cell = spread_cells(sums[...])
    lane_group = iota((N_GY, 4 * C), 1) // C
    held[...] = jnp.zeros_like(held)
    table = fz[...]
    for j in range(PAIRS):
        both = dot(table, by_cell[0][j])
        full = both[: 4 * N_GY] + both[4 * N_GY :] + dot(table[: 4 * N_GY], by_cell[1][j])
        picked = jnp.zeros((N_GY, 4 * C), F32)
        for g in range(4):
            picked = jnp.where(lane_group == g, full[g * N_GY : (g + 1) * N_GY], picked)
        held[:, j, :] = picked
    lane = iota((1, 128), 1)
    xs = jnp.zeros((1, 128), jnp.int32)
    ys = jnp.zeros((1, 128), jnp.int32)
    on = jnp.zeros((1, 128), jnp.int32)
    for j in range(PAIRS):
        b, s = divmod(j, LIST)
        here = lane == gy * PAIRS + j
        t = tile[b, s]
        xs = jnp.where(here, t // CY, xs)
        ys = jnp.where(here, CY * owner[b, s] + t % CY, ys)
        on = jnp.where(here & (s < live[b]), 1, on)
    for k, v in enumerate((xs, ys, on)):
        held[:, PAIRS + k, :] = jnp.broadcast_to(v.astype(F32), (N_GY, 128))
    sent[:, :16, :] = held[...].astype(sent.dtype)
    sent[:, 16:, :] = jnp.zeros((N_GY, BLK * NZ // 4, 4 * C), sent.dtype)
    for j in range(PAIRS):
        b, s = divmod(j, LIST)

        @pl.when(s < live[b])
        def _(b=b, s=s, j=j):
            at = 16 + b * (NZ // 4)
            rows = sums[j * (NZ // 4) : (j + 1) * (NZ // 4), :]
            sent[owner[b, s], at : at + NZ // 4, :] = rows.astype(sent.dtype)


def spread_cells(sums):
    shape = (4 * C, 16 * C)
    copy_c = (
        ((iota(shape, 0) & (C - 1)) == (iota(shape, 1) & (C - 1))) & ((iota(shape, 0) // C) == (iota(shape, 1) // (4 * C)))
    ).astype(BF16)
    terms = []
    for term in halves(sums):
        wide = dot(term, copy_c).astype(BF16)
        terms.append(
            [
                jnp.concatenate([wide[j * 32 : (j + 1) * 32, k * 128 : (k + 1) * 128] for k in range(4)], axis=0)
                for j in range(PAIRS)
            ]
        )
    return terms


def tile_kernel(slots, got, wp, bias, out, raw):
    raw[...] = jnp.zeros_like(raw)
    for n in range(N_GY * BLK):
        src, b = divmod(n, BLK)
        v = slots[0, n]

        @pl.when(v >= 0)
        def _(src=src, b=b, v=v):
            t = pl.multiple_of(v * (NZ // 4), NZ // 4)
            at = 16 + b * (NZ // 4)
            raw[pl.ds(t, NZ // 4), :] = raw[pl.ds(t, NZ // 4), :] + got[src, at : at + NZ // 4, :].astype(F32)

    pick = ((iota((4 * C, C), 0) & (C - 1)) == iota((4 * C, C), 1)).astype(BF16)
    spread = dot(dot(pick, wp[...], NT).astype(BF16), pick, NT)
    same = (iota(spread.shape, 0) // C) == (iota(spread.shape, 1) // C)
    weights = jnp.where(same, spread, 0.0).astype(BF16)
    column = jnp.broadcast_to(bias[...], (C, NZ))
    group = iota((C, NZ), 1) // (NZ // 4)
    for q in range(CX * CY // 4):
        high, low = halves(raw[q * NZ : (q + 1) * NZ, :])
        mapped = dot(weights, high, NT) + dot(weights, low, NT)
        for t in range(4):
            line = jnp.zeros((C, NZ), F32)
            for k in range(4):
                piece = mapped[k * C : (k + 1) * C]
                shift = ((k - t) * (NZ // 4)) % NZ
                line = jnp.where(group == k, piece if shift == 0 else pltpu.roll(piece, shift, 1), line)
            out[q * 4 + t] = line + column


def y_kernel(got, phase, out, slots):
    gy = lax.axis_index("gy")
    full = got[:, :16, :].astype(F32)
    values = full[:, :PAIRS, :].reshape(N_GY * PAIRS, 128)
    sent = jnp.sum(full[:, PAIRS:, :], axis=0)
    xs, ys, on = sent[0:1], sent[1:2], sent[2:3]
    square = (128, 128)
    hot = ((iota(square, 0).astype(F32) == ys) & (on > 0.5)).astype(BF16)
    turned = dot(phase[...], hot)
    here = (iota((512, 128), 0) & (CX - 1)).astype(F32) == xs
    turned = jnp.where(here, turned, 0.0).astype(BF16)
    both = dot(turned[:256], values.astype(BF16)) + dot(turned[256:], rotated(values, 1.0).astype(BF16))
    result = both[:128] + both[128:]
    out[...] = result.reshape(MODES, CX, 128).astype(out.dtype)
    yi = ys.astype(jnp.int32)
    mine = ((yi // CY) == gy) & (on > 0.5)
    number = jnp.where(mine, xs.astype(jnp.int32) * CY + (yi & (CY - 1)) + 1, 0).astype(BF16)
    group = ((iota(square, 0) // LIST) == iota(square, 1)).astype(BF16)
    slots[...] = dot(jnp.broadcast_to(number, (8, 128)), group).astype(jnp.int32) - 1


def rotated(x, sign):
    up = pltpu.roll(x, 128 - C, 1)
    down = pltpu.roll(x, C, 1)
    real = ((iota(x.shape, 1) // C) & 1) == 0
    return jnp.where(real, sign * up, -sign * down)


def x_kernel(got, weights, forward, back, out):
    size_x = CX * N_GX
    values = got[...].astype(F32).reshape(size_x, 128)
    spectrum = table_dot(forward[...], jnp.concatenate([values, rotated(values, 1.0)], axis=0))
    parts = [spectrum if g == 0 else pltpu.roll(spectrum, 128 - g * C, 1) for g in range(4)]
    high, low = halves(jnp.concatenate(parts, axis=0))
    spread = ((iota((128, C * C), 1) // C) == iota((128, C * C), 0)).astype(BF16)
    wide = dot(high, spread) + dot(low, spread)
    totals = []
    for k in range(2):
        real = wide[(2 * k) * MODES : (2 * k + 1) * MODES]
        imag = wide[(2 * k + 1) * MODES : (2 * k + 2) * MODES]
        sum_r = jnp.zeros((MODES, 128), F32)
        sum_i = jnp.zeros((MODES, 128), F32)
        for j in range(C * C // 128):
            lanes = slice(j * 128, (j + 1) * 128)
            at = (2 * k) * C * C + j * 128
            wr = weights[:, at : at + 128].astype(F32)
            wi = weights[:, at + C * C : at + C * C + 128].astype(F32)
            sum_r = sum_r + real[:, lanes] * wr - imag[:, lanes] * wi
            sum_i = sum_i + real[:, lanes] * wi + imag[:, lanes] * wr
        for v in (sum_r, sum_i):
            v = v + pltpu.roll(v, 64, 1)
            totals.append(v + pltpu.roll(v, 32, 1))
    group = iota((MODES, 128), 1) // C
    r0, i0, r1, i1 = totals
    mixed = jnp.where(group == 0, r0, jnp.where(group == 1, i0, jnp.where(group == 2, r1, i1)))
    other = jnp.where(group == 0, -i0, jnp.where(group == 1, r0, jnp.where(group == 2, -i1, r1)))
    result = table_dot(back[...], jnp.concatenate([mixed, other], axis=0))
    out[...] = result.reshape(N_GX, CX, 128).astype(out.dtype)


def back_kernel(got, back, out):
    lines = [got[:, x, :].astype(F32) for x in range(CX)]
    group = iota((MODES, 128), 1) // C
    turned = []
    for g in range(4):
        line = jnp.zeros((MODES, 128), F32)
        for x in range(CX):
            shift = ((x - g) * C) % 128
            moved = lines[x] if shift == 0 else pltpu.roll(lines[x], shift, 1)
            line = jnp.where(group == x, moved, line)
        turned.append(line)
    r0, i0, r1, i1 = turned
    stack = jnp.concatenate(
        [jnp.concatenate(turned, axis=1), jnp.concatenate([-i0, r0, -i1, r1], axis=1)], axis=0
    )
    result = table_dot(back[...], stack)
    for g in range(4):
        piece = result[:, g * 128 : (g + 1) * 128].reshape(N_GY, CY, 128)
        out[:, g * CY : (g + 1) * CY, :] = piece.astype(out.dtype)


def end_kernel(got, inverse, known, out, wide):
    wide[...] = got[...].astype(F32).reshape(N_GY * 4 * CY, 128)
    for y in range(CY):
        values = wide[pl.ds(y, 4 * N_GY, stride=CY), :].astype(BF16)
        both = dot(values, inverse[...], TN)
        line = both[:, :NZ] + both[:, NZ:]
        for x in range(CX):
            h = line[x * C : (x + 1) * C] + known[x * CY + y]
            th = jnp.tanh(h * (GELU_B * (h * h) + GELU_A))
            out[x, y] = 0.5 * (h + h * th)


def call(kernel, out_shape, in_specs, scratch=(), flops=0, size=0, vmem=8 * 1024 * 1024):
    return pl.pallas_call(
        kernel,
        out_shape=out_shape,
        in_specs=in_specs,
        scratch_shapes=list(scratch),
        compiler_params=pltpu.CompilerParams(vmem_limit_bytes=vmem),
        cost_estimate=pl.CostEstimate(flops=flops, bytes_accessed=size, transcendentals=0),
    )


VM = pl.BlockSpec(memory_space=pltpu.VMEM)
SM = pl.BlockSpec(memory_space=pltpu.SMEM)


def stage_one(
    features, offsets, point_cell, tile_owner, tile_local, live_count,
    w_first, b_first, w_second, b_second, w_third, *_,
):
    forward_z = tables(CX * N_GX, CY * N_GY)[0]
    vm = pltpu.VMEM
    return call(
        pair_kernel,
        jax.ShapeDtypeStruct((N_GY, 16 + BLK * NZ // 4, 128), BF16),
        [SM, SM, SM] + [VM] * 9,
        [
            vm((PAIRS * NZ // 4, 4 * C), F32),
            vm((NZ // 4, 4 * HID), F32), vm((NZ // 4, 4 * HID), F32),
            vm((4 * HID, 4 * HID), F32), vm((4 * HID, 4 * C), F32),
            vm((8, 4 * HID), F32), vm((BLK, PB, PB), F32), vm((BLK, PB, PB), F32),
            vm((PB, PB), F32), vm((PB, PB), F32), vm((N_GY, 16, 128), F32),
        ],
        flops=1_600_000_000, size=1_000_000, vmem=VMEM_ONE,
    )(
        tile_owner, tile_local, live_count, features, offsets, point_cell.reshape(1, -1),
        w_first.T, b_first.reshape(1, -1), b_second.reshape(1, -1), w_second, w_third, forward_z,
    )


def local(
    features, offsets, point_cell, tile_owner, tile_local, live_count,
    w_first, b_first, w_second, b_second, w_third, w_point, b_point, w_modes,
):
    _, inverse_z, phase_y, back_y, forward_x, back_x = tables(CX * N_GX, CY * N_GY)
    vm = pltpu.VMEM
    sent = stage_one(
        features, offsets, point_cell, tile_owner, tile_local, live_count,
        w_first, b_first, w_second, b_second, w_third,
    )
    sent = lax.all_to_all(sent, "gy", 0, 0, tiled=True)
    along_y, slots = call(
        y_kernel,
        (jax.ShapeDtypeStruct((MODES, CX, 128), F32), jax.ShapeDtypeStruct((8, 128), jnp.int32)),
        [VM, VM],
        flops=100_000_000, size=500_000,
    )(sent, phase_y)
    known = call(
        tile_kernel,
        jax.ShapeDtypeStruct((CX * CY, C, NZ), F32),
        [SM] + [VM] * 3,
        [vm((CX * CY * NZ // 4, 4 * C), F32)],
        flops=100_000_000, size=2_500_000,
    )(slots, sent, w_point, b_point.reshape(C, 1))
    along_y = lax.all_to_all(along_y, "gx", 0, 0, tiled=True)
    along_y, known = lax.optimization_barrier((along_y, known))
    lines = call(
        x_kernel,
        jax.ShapeDtypeStruct((N_GX, CX, 128), F32),
        [VM] * 4,
        flops=100_000_000, size=500_000,
    )(along_y, w_modes.reshape(MODES, -1), forward_x, back_x)
    lines = lax.all_to_all(lines, "gx", 0, 0, tiled=True)
    cells = call(
        back_kernel,
        jax.ShapeDtypeStruct((N_GY, 4 * CY, 128), BF16),
        [VM] * 2,
        flops=100_000_000, size=500_000,
    )(lines, back_y)
    cells = lax.all_to_all(cells, "gy", 0, 0, tiled=True)
    return call(
        end_kernel,
        jax.ShapeDtypeStruct((CX, CY, C, NZ), F32),
        [VM] * 3,
        [vm((N_GY * 4 * CY, 128), F32)],
        flops=100_000_000, size=1_000_000,
    )(cells, inverse_z, known)


def solution(mesh):
    both = ("gx", "gy")
    return jax.shard_map(
        local,
        mesh=mesh,
        in_specs=(
            P(None, both), P(None, both), P(both), P(both, None), P(both, None), P(both),
            P(), P(), P(), P(), P(), P(), P(),
            P(None, "gx", "gy", None, None, None),
        ),
        out_specs=P("gx", "gy", None, None),
        check_vma=False,
    )
```

```python
import functools
import math

import jax
import jax.numpy as jnp
import numpy as np
from jax import lax
from jax.experimental import pallas as pl
from jax.experimental.pallas import tpu as pltpu
from jax.sharding import PartitionSpec as P

NZ = 128
CX = 4
CY = 8
SPAN = 16
PB = 128
C = 32
HID = 64
N_GX = 32
N_GY = 16
BLK = 2
LIST = 4
PAIRS = BLK * LIST
MODES = 32
ANCHOR = 16
VMEM_ONE = 62 * 1024 * 1024
F32 = jnp.float32
BF16 = jnp.bfloat16
BEST = lax.Precision.HIGHEST
NN = (((1,), (0,)), ((), ()))
NT = (((1,), (1,)), ((), ()))
TN = (((0,), (0,)), ((), ()))
HALF_PI = (1.5703125, 4.837512969970703125e-4, 7.549789954891882e-8)
SIN_TERMS = (-1.9515295891e-4, 8.3321608736e-3, -1.6666654611e-1)
COS_TERMS = (2.443315711809948e-5, -1.388731625493765e-3, 4.166664568298827e-2)
GELU_A = math.sqrt(2.0 / math.pi)
GELU_B = GELU_A * 0.044715


def iota(shape, dim):
    return lax.broadcasted_iota(jnp.int32, shape, dim)


def dot(a, b, dims=NN):
    return lax.dot_general(a, b, dims, preferred_element_type=F32)


def fine_dot(a, b, dims=NN):
    return lax.dot_general(a, b, dims, precision=BEST, preferred_element_type=F32)


def halves(x):
    high = x.astype(BF16)
    return high, (x - high.astype(F32)).astype(BF16)


def table_dot(table, x):
    high, low = halves(x)
    rows = table.shape[0] // 2
    both = dot(table, high)
    return both[:rows] + both[rows:] + dot(table[:rows], low)


def sin_cos(x):
    count = jnp.floor(x * (2.0 / math.pi) + 0.5)
    rest = x - count * HALF_PI[0]
    rest = rest - count * HALF_PI[1]
    rest = rest - count * HALF_PI[2]
    square = rest * rest
    s = (SIN_TERMS[0] * square + SIN_TERMS[1]) * square + SIN_TERMS[2]
    s = s * square * rest + rest
    c = (COS_TERMS[0] * square + COS_TERMS[1]) * square + COS_TERMS[2]
    c = c * square * square - 0.5 * square + 1.0
    quarter = count.astype(jnp.int32)
    odd = (quarter & 1) != 0
    sine = jnp.where(odd, c, s)
    cosine = jnp.where(odd, s, c)
    sine = jnp.where((quarter & 2) != 0, -sine, sine)
    cosine = jnp.where(((quarter + 1) & 2) != 0, -cosine, cosine)
    return sine, cosine


def angles(length, two_sided):
    orders = np.arange(MODES)
    frequency = np.where(orders < MODES // 2, orders, length - MODES + orders) if two_sided else orders
    turns = np.arange(length)[:, None] * frequency[None, :] % length
    return turns * (2.0 * math.pi / length)


def f32(x):
    return np.ascontiguousarray(x, dtype=np.float32)


def split_table(x):
    high = f32(x).astype(jnp.bfloat16)
    low = (x - high.astype(np.float64)).astype(np.float32).astype(jnp.bfloat16)
    return high, low


def tables(size_x, size_y):
    scale = 1.0 / math.sqrt(size_x * size_y * NZ)
    along_z = angles(NZ, False)
    both = np.stack([np.cos(along_z), -np.sin(along_z)], -1) * scale
    both = both.reshape(NZ, N_GY, 4)
    forward_z = np.concatenate(split_table(both.transpose(2, 1, 0).reshape(4 * N_GY, NZ)), 0)
    inverse_z = np.concatenate(split_table(both.reshape(NZ, 4 * N_GY).T), 1)
    along_y = angles(size_y, True)
    per_row = np.repeat(along_y.T, CX, axis=0)
    phase_y = np.concatenate(split_table(np.cos(per_row)) + split_table(np.sin(per_row)), 0)
    back_y = np.concatenate(split_table(np.concatenate([np.cos(along_y), np.sin(along_y)], 1)), 0)
    along_x = angles(size_x, True)
    forward_x = np.concatenate(split_table(np.concatenate([np.cos(along_x), np.sin(along_x)], 0).T), 0)
    back_x = np.concatenate(split_table(np.concatenate([np.cos(along_x), np.sin(along_x)], 1)), 0)
    return forward_z, inverse_z, phase_y, back_y, forward_x, back_x


def pair_kernel(
    owner, tile, live, feats, offs, cells, w1, b1, b2, w2, w3, fz,
    sent,
    sums, cz, sz, w2b, w3b, side, point, feat, sin_p, cos_p, held,
):
    gx = lax.axis_index("gx")
    gy = lax.axis_index("gy")
    pick = ((iota((4 * HID, HID), 0) & (HID - 1)) == iota((4 * HID, HID), 1)).astype(BF16)
    spread = dot(dot(pick, w2[...], NT).astype(BF16), pick, NT)
    same = (iota(spread.shape, 0) // HID) == (iota(spread.shape, 1) // HID)
    w2b[...] = jnp.where(same, spread, 0.0)
    pick_c = ((iota((4 * C, C), 0) & (C - 1)) == iota((4 * C, C), 1)).astype(BF16)
    spread = dot(dot(pick, w3[...], NT).astype(BF16), pick_c, NT)
    same = (iota(spread.shape, 0) // HID) == (iota(spread.shape, 1) // C)
    w3b[...] = jnp.where(same, 0.5 * spread, 0.0)
    shape = (HID, 4 * HID)
    pick_t = (iota(shape, 0) == (iota(shape, 1) & (HID - 1))).astype(F32)
    side[0:3, :] = fine_dot(w1[...].astype(F32), pick_t)
    side[3:4, :] = fine_dot(jnp.broadcast_to(b1[...], (8, HID)), pick_t)[0:1]
    side[4:5, :] = fine_dot(jnp.broadcast_to(b2[...], (8, HID)), pick_t)[0:1]
    cell_z = ((iota((NZ // 4, 4 * HID), 1) // HID) * (NZ // 4) + iota((NZ // 4, 4 * HID), 0)).astype(F32)
    sine, cosine = sin_cos(side[2:3, :] * cell_z)
    cz[...] = cosine
    sz[...] = sine
    side[5:6, :] = 2.0 * sin_cos(jnp.broadcast_to(side[2:3, :], (8, 4 * HID)))[1][0:1]
    sums[...] = jnp.zeros_like(sums)
    row_of = iota((PB, PB), 0)
    for b in range(BLK):
        span = slice(b * PB, (b + 1) * PB)
        q = cells[:, span]
        place = [
            ((q // 64) * SPAN).astype(F32) + offs[0:1, span].astype(F32),
            ((q // 8 % 8) * SPAN).astype(F32) + offs[1:2, span].astype(F32),
            ((q % 8) * SPAN).astype(F32) + offs[2:3, span].astype(F32),
        ]
        stack = jnp.where(row_of == 0, place[0], jnp.where(row_of == 1, place[1], place[2]))
        turned = jnp.transpose(stack)
        point[b] = (
            turned[:, 0:1] * side[0:1, :PB] + turned[:, 1:2] * side[1:2, :PB] + turned[:, 2:3] * side[2:3, :PB]
        )
        block = feats[:, span].astype(F32) * (1.0 / math.sqrt(PB))
        feat[b] = jnp.transpose(jnp.concatenate([block] * 4, axis=0))
    for b in range(BLK):

        def one_pair(s, carry, b=b):
            t = tile[b, s]
            x = (CX * gx + t // CY).astype(F32)
            y = (CY * owner[b, s] + t % CY).astype(F32)
            line = side[0:1, :PB] * x + side[1:2, :PB] * y + side[3:4, :PB]
            sine, cosine = sin_cos(line - point[b])
            sin_p[...] = sine
            cos_p[...] = cosine
            twice = side[5:6, :PB]

            lines = []
            for g in range(NZ // 4):
                if g % ANCHOR < 2:
                    sp = sin_p[...]
                    cp = cos_p[...]
                    c = cz[g : g + 1, :]
                    d = sz[g : g + 1, :]
                    now = sp * c[:, :PB] + cp * d[:, :PB], sp * c[:, PB:] + cp * d[:, PB:]
                else:
                    now = twice * last[0] - before[0], twice * last[1] - before[1]
                if g % ANCHOR:
                    before = last
                last = now
                lines.append(jnp.concatenate(now, axis=1))
            h = dot(jnp.concatenate(lines, axis=0), w2b[...]) + side[4:5, :]
            th = jnp.tanh(h * (GELU_B * (h * h) + GELU_A))
            kern = dot(h + h * th, w3b[...])
            for g in range(NZ // 4):
                total = jnp.sum(kern[g * PB : (g + 1) * PB] * feat[b], axis=0, keepdims=True)
                sums[pl.ds((b * LIST + s) * (NZ // 4) + g, 1), :] = total
            return carry

        lax.fori_loop(0, live[b], one_pair, 0)
    by_cell = spread_cells(sums[...])
    lane_group = iota((N_GY, 4 * C), 1) // C
    held[...] = jnp.zeros_like(held)
    table = fz[...]
    for j in range(PAIRS):
        both = dot(table, by_cell[0][j])
        full = both[: 4 * N_GY] + both[4 * N_GY :] + dot(table[: 4 * N_GY], by_cell[1][j])
        picked = jnp.zeros((N_GY, 4 * C), F32)
        for g in range(4):
            picked = jnp.where(lane_group == g, full[g * N_GY : (g + 1) * N_GY], picked)
        held[:, j, :] = picked
    lane = iota((1, 128), 1)
    xs = jnp.zeros((1, 128), jnp.int32)
    ys = jnp.zeros((1, 128), jnp.int32)
    on = jnp.zeros((1, 128), jnp.int32)
    for j in range(PAIRS):
        b, s = divmod(j, LIST)
        here = lane == gy * PAIRS + j
        t = tile[b, s]
        xs = jnp.where(here, t // CY, xs)
        ys = jnp.where(here, CY * owner[b, s] + t % CY, ys)
        on = jnp.where(here & (s < live[b]), 1, on)
    for k, v in enumerate((xs, ys, on)):
        held[:, PAIRS + k, :] = jnp.broadcast_to(v.astype(F32), (N_GY, 128))
    sent[:, :16, :] = held[...].astype(sent.dtype)
    sent[:, 16:, :] = jnp.zeros((N_GY, BLK * NZ // 4, 4 * C), sent.dtype)
    for j in range(PAIRS):
        b, s = divmod(j, LIST)

        @pl.when(s < live[b])
        def _(b=b, s=s, j=j):
            at = 16 + b * (NZ // 4)
            rows = sums[j * (NZ // 4) : (j + 1) * (NZ // 4), :]
            sent[owner[b, s], at : at + NZ // 4, :] = rows.astype(sent.dtype)


def spread_cells(sums):
    shape = (4 * C, 16 * C)
    copy_c = (
        ((iota(shape, 0) & (C - 1)) == (iota(shape, 1) & (C - 1))) & ((iota(shape, 0) // C) == (iota(shape, 1) // (4 * C)))
    ).astype(BF16)
    terms = []
    for term in halves(sums):
        wide = dot(term, copy_c).astype(BF16)
        terms.append(
            [
                jnp.concatenate([wide[j * 32 : (j + 1) * 32, k * 128 : (k + 1) * 128] for k in range(4)], axis=0)
                for j in range(PAIRS)
            ]
        )
    return terms


def tile_kernel(slots, got, wp, bias, out, raw):
    raw[...] = jnp.zeros_like(raw)
    for n in range(N_GY * BLK):
        src, b = divmod(n, BLK)
        v = slots[0, n]

        @pl.when(v >= 0)
        def _(src=src, b=b, v=v):
            t = pl.multiple_of(v * (NZ // 4), NZ // 4)
            at = 16 + b * (NZ // 4)
            raw[pl.ds(t, NZ // 4), :] = raw[pl.ds(t, NZ // 4), :] + got[src, at : at + NZ // 4, :].astype(F32)

    pick = ((iota((4 * C, C), 0) & (C - 1)) == iota((4 * C, C), 1)).astype(BF16)
    spread = dot(dot(pick, wp[...], NT).astype(BF16), pick, NT)
    same = (iota(spread.shape, 0) // C) == (iota(spread.shape, 1) // C)
    weights = jnp.where(same, spread, 0.0).astype(BF16)
    column = jnp.broadcast_to(bias[...], (C, NZ))
    group = iota((C, NZ), 1) // (NZ // 4)
    for q in range(CX * CY // 4):
        high, low = halves(raw[q * NZ : (q + 1) * NZ, :])
        mapped = dot(weights, high, NT) + dot(weights, low, NT)
        for t in range(4):
            line = jnp.zeros((C, NZ), F32)
            for k in range(4):
                piece = mapped[k * C : (k + 1) * C]
                shift = ((k - t) * (NZ // 4)) % NZ
                line = jnp.where(group == k, piece if shift == 0 else pltpu.roll(piece, shift, 1), line)
            out[q * 4 + t] = line + column


def y_kernel(got, phase, out, slots):
    gy = lax.axis_index("gy")
    full = got[:, :16, :].astype(F32)
    values = full[:, :PAIRS, :].reshape(N_GY * PAIRS, 128)
    sent = jnp.sum(full[:, PAIRS:, :], axis=0)
    xs, ys, on = sent[0:1], sent[1:2], sent[2:3]
    square = (128, 128)
    hot = ((iota(square, 0).astype(F32) == ys) & (on > 0.5)).astype(BF16)
    turned = dot(phase[...], hot)
    here = (iota((512, 128), 0) & (CX - 1)).astype(F32) == xs
    turned = jnp.where(here, turned, 0.0).astype(BF16)
    turned = jnp.concatenate([turned[:256], turned[256:]], axis=1)
    both = dot(turned, jnp.concatenate([values, rotated(values, 1.0)], axis=0).astype(BF16))
    result = both[:128] + both[128:]
    out[...] = result.reshape(MODES, CX, 128).astype(out.dtype)
    yi = ys.astype(jnp.int32)
    mine = ((yi // CY) == gy) & (on > 0.5)
    number = jnp.where(mine, xs.astype(jnp.int32) * CY + (yi & (CY - 1)) + 1, 0).astype(BF16)
    group = ((iota(square, 0) // LIST) == iota(square, 1)).astype(BF16)
    slots[...] = dot(jnp.broadcast_to(number, (8, 128)), group).astype(jnp.int32) - 1


def rotated(x, sign):
    up = pltpu.roll(x, 128 - C, 1)
    down = pltpu.roll(x, C, 1)
    real = ((iota(x.shape, 1) // C) & 1) == 0
    return jnp.where(real, sign * up, -sign * down)


def x_kernel(got, weights, forward, back, out):
    size_x = CX * N_GX
    values = got[...].astype(F32).reshape(size_x, 128)
    spectrum = table_dot(forward[...], jnp.concatenate([values, rotated(values, 1.0)], axis=0))
    parts = [spectrum if g == 0 else pltpu.roll(spectrum, 128 - g * C, 1) for g in range(4)]
    terms = jnp.concatenate(halves(jnp.concatenate(parts, axis=0)), axis=1)
    spread = ((iota((256, C * C), 1) // C) == (iota((256, C * C), 0) & 127)).astype(BF16)
    wide = dot(terms, spread)
    totals = []
    for k in range(2):
        real = wide[(2 * k) * MODES : (2 * k + 1) * MODES]
        imag = wide[(2 * k + 1) * MODES : (2 * k + 2) * MODES]
        sum_r = jnp.zeros((MODES, 128), F32)
        sum_i = jnp.zeros((MODES, 128), F32)
        for j in range(C * C // 128):
            lanes = slice(j * 128, (j + 1) * 128)
            at = (2 * k) * C * C + j * 128
            wr = weights[:, at : at + 128].astype(F32)
            wi = weights[:, at + C * C : at + C * C + 128].astype(F32)
            sum_r = sum_r + real[:, lanes] * wr - imag[:, lanes] * wi
            sum_i = sum_i + real[:, lanes] * wi + imag[:, lanes] * wr
        for v in (sum_r, sum_i):
            v = v + pltpu.roll(v, 64, 1)
            totals.append(v + pltpu.roll(v, 32, 1))
    group = iota((MODES, 128), 1) // C
    r0, i0, r1, i1 = totals
    mixed = jnp.where(group == 0, r0, jnp.where(group == 1, i0, jnp.where(group == 2, r1, i1)))
    other = jnp.where(group == 0, -i0, jnp.where(group == 1, r0, jnp.where(group == 2, -i1, r1)))
    result = table_dot(back[...], jnp.concatenate([mixed, other], axis=0))
    out[...] = result.reshape(N_GX, CX, 128).astype(out.dtype)


def back_kernel(got, back, out):
    lines = [got[:, x, :].astype(F32) for x in range(CX)]
    group = iota((MODES, 128), 1) // C
    turned = []
    for g in range(4):
        line = jnp.zeros((MODES, 128), F32)
        for x in range(CX):
            shift = ((x - g) * C) % 128
            moved = lines[x] if shift == 0 else pltpu.roll(lines[x], shift, 1)
            line = jnp.where(group == x, moved, line)
        turned.append(line)
    r0, i0, r1, i1 = turned
    stack = jnp.concatenate(
        [jnp.concatenate(turned, axis=1), jnp.concatenate([-i0, r0, -i1, r1], axis=1)], axis=0
    )
    result = table_dot(back[...], stack)
    for g in range(4):
        piece = result[:, g * 128 : (g + 1) * 128].reshape(N_GY, CY, 128)
        out[:, g * CY : (g + 1) * CY, :] = piece.astype(out.dtype)


def end_kernel(got, inverse, known, out, wide, done, sent):
    wide[...] = got[...].astype(F32).reshape(N_GY * 4 * CY, 128)
    copies = []
    for y in range(CY):
        values = wide[pl.ds(y, 4 * N_GY, stride=CY), :].astype(BF16)
        both = dot(values, inverse[...], TN)
        line = both[:, :NZ] + both[:, NZ:]
        for x in range(CX):
            h = line[x * C : (x + 1) * C] + known[x * CY + y]
            th = jnp.tanh(h * (GELU_B * (h * h) + GELU_A))
            done[y, x] = 0.5 * (h + h * th)
        copies.append(pltpu.make_async_copy(done.at[y], out.at[:, y], sent.at[y]))
        copies[-1].start()
    for copy in copies:
        copy.wait()


def call(kernel, out_shape, in_specs, scratch=(), flops=0, size=0, vmem=8 * 1024 * 1024, out=None):
    return pl.pallas_call(
        kernel,
        out_shape=out_shape,
        in_specs=in_specs,
        **({} if out is None else {"out_specs": out}),
        scratch_shapes=list(scratch),
        compiler_params=pltpu.CompilerParams(vmem_limit_bytes=vmem),
        cost_estimate=pl.CostEstimate(flops=flops, bytes_accessed=size, transcendentals=0),
    )


VM = pl.BlockSpec(memory_space=pltpu.VMEM)
SM = pl.BlockSpec(memory_space=pltpu.SMEM)


def stage_one(
    features, offsets, point_cell, tile_owner, tile_local, live_count,
    w_first, b_first, w_second, b_second, w_third, *_,
):
    forward_z = tables(CX * N_GX, CY * N_GY)[0]
    vm = pltpu.VMEM
    return call(
        pair_kernel,
        jax.ShapeDtypeStruct((N_GY, 16 + BLK * NZ // 4, 128), BF16),
        [SM, SM, SM] + [VM] * 9,
        [
            vm((PAIRS * NZ // 4, 4 * C), F32),
            vm((NZ // 4, 4 * HID), F32), vm((NZ // 4, 4 * HID), F32),
            vm((4 * HID, 4 * HID), F32), vm((4 * HID, 4 * C), F32),
            vm((8, 4 * HID), F32), vm((BLK, PB, PB), F32), vm((BLK, PB, PB), F32),
            vm((PB, PB), F32), vm((PB, PB), F32), vm((N_GY, 16, 128), F32),
        ],
        flops=1_600_000_000, size=1_000_000, vmem=VMEM_ONE,
    )(
        tile_owner, tile_local, live_count, features, offsets, point_cell.reshape(1, -1),
        w_first.T, b_first.reshape(1, -1), b_second.reshape(1, -1), w_second, w_third, forward_z,
    )


def local(
    features, offsets, point_cell, tile_owner, tile_local, live_count,
    w_first, b_first, w_second, b_second, w_third, w_point, b_point, w_modes,
):
    _, inverse_z, phase_y, back_y, forward_x, back_x = tables(CX * N_GX, CY * N_GY)
    vm = pltpu.VMEM
    sent = stage_one(
        features, offsets, point_cell, tile_owner, tile_local, live_count,
        w_first, b_first, w_second, b_second, w_third,
    )
    sent = lax.all_to_all(sent, "gy", 0, 0, tiled=True)
    along_y, slots = call(
        y_kernel,
        (jax.ShapeDtypeStruct((MODES, CX, 128), F32), jax.ShapeDtypeStruct((8, 128), jnp.int32)),
        [VM, VM],
        flops=100_000_000, size=500_000,
    )(sent, phase_y)
    known = call(
        tile_kernel,
        jax.ShapeDtypeStruct((CX * CY, C, NZ), F32),
        [SM] + [VM] * 3,
        [vm((CX * CY * NZ // 4, 4 * C), F32)],
        flops=100_000_000, size=2_500_000,
    )(slots, sent, w_point, b_point.reshape(C, 1))
    along_y = lax.all_to_all(along_y, "gx", 0, 0, tiled=True)
    along_y, known = lax.optimization_barrier((along_y, known))
    lines = call(
        x_kernel,
        jax.ShapeDtypeStruct((N_GX, CX, 128), F32),
        [VM] * 4,
        flops=100_000_000, size=500_000,
    )(along_y, w_modes.reshape(MODES, -1), forward_x, back_x)
    lines = lax.all_to_all(lines, "gx", 0, 0, tiled=True)
    cells = call(
        back_kernel,
        jax.ShapeDtypeStruct((N_GY, 4 * CY, 128), BF16),
        [VM] * 2,
        flops=100_000_000, size=500_000,
    )(lines, back_y)
    cells = lax.all_to_all(cells, "gy", 0, 0, tiled=True)
    return call(
        end_kernel,
        jax.ShapeDtypeStruct((CX, CY, C, NZ), F32),
        [VM] * 3,
        [vm((N_GY * 4 * CY, 128), F32), vm((CY, CX, C, NZ), F32), pltpu.SemaphoreType.DMA((CY,))],
        flops=100_000_000, size=1_000_000, out=pl.BlockSpec(memory_space=pl.ANY),
    )(cells, inverse_z, known)


def solution(mesh):
    both = ("gx", "gy")
    return jax.shard_map(
        local,
        mesh=mesh,
        in_specs=(
            P(None, both), P(None, both), P(both), P(both, None), P(both, None), P(both),
            P(), P(), P(), P(), P(), P(), P(),
            P(None, "gx", "gy", None, None, None),
        ),
        out_specs=P("gx", "gy", None, None),
        check_vma=False,
    )
```

```python
import functools
import math

import jax
import jax.numpy as jnp
import numpy as np
from jax import lax
from jax.experimental import pallas as pl
from jax.experimental.pallas import tpu as pltpu
from jax.sharding import PartitionSpec as P

NZ = 128
CX = 4
CY = 8
SPAN = 16
PB = 128
C = 32
HID = 64
N_GX = 32
N_GY = 16
BLK = 2
LIST = 4
PAIRS = BLK * LIST
MODES = 32
ANCHOR = 32
VMEM_ONE = 62 * 1024 * 1024
F32 = jnp.float32
BF16 = jnp.bfloat16
BEST = lax.Precision.HIGHEST
NN = (((1,), (0,)), ((), ()))
NT = (((1,), (1,)), ((), ()))
TN = (((0,), (0,)), ((), ()))
HALF_PI = (1.5703125, 4.837512969970703125e-4, 7.549789954891882e-8)
SIN_TERMS = (-1.9515295891e-4, 8.3321608736e-3, -1.6666654611e-1)
COS_TERMS = (2.443315711809948e-5, -1.388731625493765e-3, 4.166664568298827e-2)
GELU_A = math.sqrt(2.0 / math.pi)
GELU_B = GELU_A * 0.044715


def iota(shape, dim):
    return lax.broadcasted_iota(jnp.int32, shape, dim)


def dot(a, b, dims=NN):
    return lax.dot_general(a, b, dims, preferred_element_type=F32)


def fine_dot(a, b, dims=NN):
    return lax.dot_general(a, b, dims, precision=BEST, preferred_element_type=F32)


def halves(x):
    high = x.astype(BF16)
    return high, (x - high.astype(F32)).astype(BF16)


def table_dot(table, x):
    high, low = halves(x)
    rows = table.shape[0] // 2
    both = dot(table, high)
    return both[:rows] + both[rows:] + dot(table[:rows], low)


def sin_cos(x):
    count = jnp.floor(x * (2.0 / math.pi) + 0.5)
    rest = x - count * HALF_PI[0]
    rest = rest - count * HALF_PI[1]
    rest = rest - count * HALF_PI[2]
    square = rest * rest
    s = (SIN_TERMS[0] * square + SIN_TERMS[1]) * square + SIN_TERMS[2]
    s = s * square * rest + rest
    c = (COS_TERMS[0] * square + COS_TERMS[1]) * square + COS_TERMS[2]
    c = c * square * square - 0.5 * square + 1.0
    quarter = count.astype(jnp.int32)
    odd = (quarter & 1) != 0
    sine = jnp.where(odd, c, s)
    cosine = jnp.where(odd, s, c)
    sine = jnp.where((quarter & 2) != 0, -sine, sine)
    cosine = jnp.where(((quarter + 1) & 2) != 0, -cosine, cosine)
    return sine, cosine


def angles(length, two_sided):
    orders = np.arange(MODES)
    frequency = np.where(orders < MODES // 2, orders, length - MODES + orders) if two_sided else orders
    turns = np.arange(length)[:, None] * frequency[None, :] % length
    return turns * (2.0 * math.pi / length)


def f32(x):
    return np.ascontiguousarray(x, dtype=np.float32)


def split_table(x):
    high = f32(x).astype(jnp.bfloat16)
    low = (x - high.astype(np.float64)).astype(np.float32).astype(jnp.bfloat16)
    return high, low


def tables(size_x, size_y):
    scale = 1.0 / math.sqrt(size_x * size_y * NZ)
    along_z = angles(NZ, False)
    both = np.stack([np.cos(along_z), -np.sin(along_z)], -1) * scale
    both = both.reshape(NZ, N_GY, 4)
    forward_z = np.concatenate(split_table(both.transpose(2, 1, 0).reshape(4 * N_GY, NZ)), 0)
    inverse_z = np.concatenate(split_table(both.reshape(NZ, 4 * N_GY).T), 1)
    along_y = angles(size_y, True)
    per_row = np.repeat(along_y.T, CX, axis=0)
    phase_y = np.concatenate(split_table(np.cos(per_row)) + split_table(np.sin(per_row)), 0)
    back_y = np.concatenate(split_table(np.concatenate([np.cos(along_y), np.sin(along_y)], 1)), 0)
    along_x = angles(size_x, True)
    forward_x = np.concatenate(split_table(np.concatenate([np.cos(along_x), np.sin(along_x)], 0).T), 0)
    back_x = np.concatenate(split_table(np.concatenate([np.cos(along_x), np.sin(along_x)], 1)), 0)
    return forward_z, inverse_z, phase_y, back_y, forward_x, back_x


def pair_kernel(
    owner, tile, live, feats, offs, cells, w1, b1, b2, w2, w3, fz,
    sent,
    sums, cz, sz, w2b, w3b, side, point, feat, sin_p, cos_p, held,
):
    gx = lax.axis_index("gx")
    gy = lax.axis_index("gy")
    pick = ((iota((4 * HID, HID), 0) & (HID - 1)) == iota((4 * HID, HID), 1)).astype(BF16)
    spread = dot(dot(pick, w2[...], NT).astype(BF16), pick, NT)
    same = (iota(spread.shape, 0) // HID) == (iota(spread.shape, 1) // HID)
    w2b[...] = jnp.where(same, spread, 0.0)
    pick_c = ((iota((4 * C, C), 0) & (C - 1)) == iota((4 * C, C), 1)).astype(BF16)
    spread = dot(dot(pick, w3[...], NT).astype(BF16), pick_c, NT)
    same = (iota(spread.shape, 0) // HID) == (iota(spread.shape, 1) // C)
    w3b[...] = jnp.where(same, 0.5 * spread, 0.0)
    shape = (HID, 4 * HID)
    pick_t = (iota(shape, 0) == (iota(shape, 1) & (HID - 1))).astype(F32)
    side[0:3, :] = fine_dot(w1[...].astype(F32), pick_t)
    side[3:4, :] = fine_dot(jnp.broadcast_to(b1[...], (8, HID)), pick_t)[0:1]
    side[4:5, :] = fine_dot(jnp.broadcast_to(b2[...], (8, HID)), pick_t)[0:1]
    cell_z = ((iota((NZ // 4, 4 * HID), 1) // HID) * (NZ // 4) + iota((NZ // 4, 4 * HID), 0)).astype(F32)
    sine, cosine = sin_cos(side[2:3, :] * cell_z)
    cz[...] = cosine
    sz[...] = sine
    side[5:6, :] = 2.0 * sin_cos(jnp.broadcast_to(side[2:3, :], (8, 4 * HID)))[1][0:1]
    sums[...] = jnp.zeros_like(sums)
    row_of = iota((PB, PB), 0)
    for b in range(BLK):
        span = slice(b * PB, (b + 1) * PB)
        q = cells[:, span]
        place = [
            ((q // 64) * SPAN).astype(F32) + offs[0:1, span].astype(F32),
            ((q // 8 % 8) * SPAN).astype(F32) + offs[1:2, span].astype(F32),
            ((q % 8) * SPAN).astype(F32) + offs[2:3, span].astype(F32),
        ]
        stack = jnp.where(row_of == 0, place[0], jnp.where(row_of == 1, place[1], place[2]))
        turned = jnp.transpose(stack)
        point[b] = (
            turned[:, 0:1] * side[0:1, :PB] + turned[:, 1:2] * side[1:2, :PB] + turned[:, 2:3] * side[2:3, :PB]
        )
        block = feats[:, span].astype(F32) * (1.0 / math.sqrt(PB))
        feat[b] = jnp.transpose(jnp.concatenate([block] * 4, axis=0))
    for b in range(BLK):

        def one_pair(s, carry, b=b):
            t = tile[b, s]
            x = (CX * gx + t // CY).astype(F32)
            y = (CY * owner[b, s] + t % CY).astype(F32)
            line = side[0:1, :PB] * x + side[1:2, :PB] * y + side[3:4, :PB]
            sine, cosine = sin_cos(line - point[b])
            sin_p[...] = sine
            cos_p[...] = cosine
            twice = side[5:6, :PB]

            lines = []
            for g in range(NZ // 4):
                if g % ANCHOR < 2:
                    sp = sin_p[...]
                    cp = cos_p[...]
                    c = cz[g : g + 1, :]
                    d = sz[g : g + 1, :]
                    now = sp * c[:, :PB] + cp * d[:, :PB], sp * c[:, PB:] + cp * d[:, PB:]
                else:
                    now = twice * last[0] - before[0], twice * last[1] - before[1]
                if g % ANCHOR:
                    before = last
                last = now
                lines.append(jnp.concatenate(now, axis=1))
            h = dot(jnp.concatenate(lines, axis=0), w2b[...]) + side[4:5, :]
            th = jnp.tanh(h * (GELU_B * (h * h) + GELU_A))
            kern = dot(h + h * th, w3b[...])
            for g in range(NZ // 4):
                total = jnp.sum(kern[g * PB : (g + 1) * PB] * feat[b], axis=0, keepdims=True)
                sums[pl.ds((b * LIST + s) * (NZ // 4) + g, 1), :] = total
            return carry

        lax.fori_loop(0, live[b], one_pair, 0)
    by_cell = spread_cells(sums[...])
    lane_group = iota((N_GY, 4 * C), 1) // C
    held[...] = jnp.zeros_like(held)
    table = fz[...]
    for j in range(0, PAIRS, 2):
        high, low = (jnp.concatenate(term[j : j + 2], axis=1) for term in by_cell)
        both = dot(table, high)
        full = both[: 4 * N_GY] + both[4 * N_GY :] + dot(table[: 4 * N_GY], low)
        for k in range(2):
            picked = jnp.zeros((N_GY, 4 * C), F32)
            for g in range(4):
                part = full[g * N_GY : (g + 1) * N_GY, k * 4 * C : (k + 1) * 4 * C]
                picked = jnp.where(lane_group == g, part, picked)
            held[:, j + k, :] = picked
    lane = iota((1, 128), 1)
    xs = jnp.zeros((1, 128), jnp.int32)
    ys = jnp.zeros((1, 128), jnp.int32)
    on = jnp.zeros((1, 128), jnp.int32)
    for j in range(PAIRS):
        b, s = divmod(j, LIST)
        here = lane == gy * PAIRS + j
        t = tile[b, s]
        xs = jnp.where(here, t // CY, xs)
        ys = jnp.where(here, CY * owner[b, s] + t % CY, ys)
        on = jnp.where(here & (s < live[b]), 1, on)
    for k, v in enumerate((xs, ys, on)):
        held[:, PAIRS + k, :] = jnp.broadcast_to(v.astype(F32), (N_GY, 128))
    sent[:, :16, :] = held[...].astype(sent.dtype)
    sent[:, 16:, :] = jnp.zeros((N_GY, BLK * NZ // 4, 4 * C), sent.dtype)
    for j in range(PAIRS):
        b, s = divmod(j, LIST)

        @pl.when(s < live[b])
        def _(b=b, s=s, j=j):
            at = 16 + b * (NZ // 4)
            rows = sums[j * (NZ // 4) : (j + 1) * (NZ // 4), :]
            sent[owner[b, s], at : at + NZ // 4, :] = rows.astype(sent.dtype)


def spread_cells(sums):
    shape = (4 * C, 16 * C)
    copy_c = (
        ((iota(shape, 0) & (C - 1)) == (iota(shape, 1) & (C - 1))) & ((iota(shape, 0) // C) == (iota(shape, 1) // (4 * C)))
    ).astype(BF16)
    terms = []
    for term in halves(sums):
        wide = dot(term, copy_c).astype(BF16)
        terms.append(
            [
                jnp.concatenate([wide[j * 32 : (j + 1) * 32, k * 128 : (k + 1) * 128] for k in range(4)], axis=0)
                for j in range(PAIRS)
            ]
        )
    return terms


def tile_kernel(slots, got, wp, bias, out, raw):
    raw[...] = jnp.zeros_like(raw)
    for n in range(N_GY * BLK):
        src, b = divmod(n, BLK)
        v = slots[0, n]

        @pl.when(v >= 0)
        def _(src=src, b=b, v=v):
            t = pl.multiple_of(v * (NZ // 4), NZ // 4)
            at = 16 + b * (NZ // 4)
            raw[pl.ds(t, NZ // 4), :] = raw[pl.ds(t, NZ // 4), :] + got[src, at : at + NZ // 4, :].astype(F32)

    pick = ((iota((4 * C, C), 0) & (C - 1)) == iota((4 * C, C), 1)).astype(BF16)
    spread = dot(dot(pick, wp[...], NT).astype(BF16), pick, NT)
    same = (iota(spread.shape, 0) // C) == (iota(spread.shape, 1) // C)
    weights = jnp.where(same, spread, 0.0).astype(BF16)
    column = jnp.broadcast_to(bias[...], (C, NZ))
    group = iota((C, NZ), 1) // (NZ // 4)
    for q in range(CX * CY // 4):
        high, low = halves(raw[q * NZ : (q + 1) * NZ, :])
        mapped = dot(weights, high, NT) + dot(weights, low, NT)
        for t in range(4):
            line = jnp.zeros((C, NZ), F32)
            for k in range(4):
                piece = mapped[k * C : (k + 1) * C]
                shift = ((k - t) * (NZ // 4)) % NZ
                line = jnp.where(group == k, piece if shift == 0 else pltpu.roll(piece, shift, 1), line)
            out[q * 4 + t] = line + column


def y_kernel(got, phase, out, slots):
    gy = lax.axis_index("gy")
    full = got[:, :16, :].astype(F32)
    values = full[:, :PAIRS, :].reshape(N_GY * PAIRS, 128)
    sent = jnp.sum(full[:, PAIRS:, :], axis=0)
    xs, ys, on = sent[0:1], sent[1:2], sent[2:3]
    square = (128, 128)
    hot = ((iota(square, 0).astype(F32) == ys) & (on > 0.5)).astype(BF16)
    turned = dot(phase[...], hot)
    here = (iota((512, 128), 0) & (CX - 1)).astype(F32) == xs
    turned = jnp.where(here, turned, 0.0).astype(BF16)
    turned = jnp.concatenate([turned[:256], turned[256:]], axis=1)
    both = dot(turned, jnp.concatenate([values, rotated(values, 1.0)], axis=0).astype(BF16))
    result = both[:128] + both[128:]
    out[...] = result.reshape(MODES, CX, 128).astype(out.dtype)
    yi = ys.astype(jnp.int32)
    mine = ((yi // CY) == gy) & (on > 0.5)
    number = jnp.where(mine, xs.astype(jnp.int32) * CY + (yi & (CY - 1)) + 1, 0).astype(BF16)
    group = ((iota(square, 0) // LIST) == iota(square, 1)).astype(BF16)
    slots[...] = dot(jnp.broadcast_to(number, (8, 128)), group).astype(jnp.int32) - 1


def rotated(x, sign):
    up = pltpu.roll(x, 128 - C, 1)
    down = pltpu.roll(x, C, 1)
    real = ((iota(x.shape, 1) // C) & 1) == 0
    return jnp.where(real, sign * up, -sign * down)


def x_kernel(got, weights, forward, back, out):
    size_x = CX * N_GX
    values = got[...].astype(F32).reshape(size_x, 128)
    spectrum = table_dot(forward[...], jnp.concatenate([values, rotated(values, 1.0)], axis=0))
    parts = [spectrum if g == 0 else pltpu.roll(spectrum, 128 - g * C, 1) for g in range(4)]
    terms = jnp.concatenate(halves(jnp.concatenate(parts, axis=0)), axis=1)
    spread = ((iota((256, C * C), 1) // C) == (iota((256, C * C), 0) & 127)).astype(BF16)
    wide = dot(terms, spread)
    totals = []
    for k in range(2):
        real = wide[(2 * k) * MODES : (2 * k + 1) * MODES]
        imag = wide[(2 * k + 1) * MODES : (2 * k + 2) * MODES]
        sum_r = jnp.zeros((MODES, 128), F32)
        sum_i = jnp.zeros((MODES, 128), F32)
        for j in range(C * C // 128):
            lanes = slice(j * 128, (j + 1) * 128)
            at = (2 * k) * C * C + j * 128
            wr = weights[:, at : at + 128].astype(F32)
            wi = weights[:, at + C * C : at + C * C + 128].astype(F32)
            sum_r = sum_r + real[:, lanes] * wr - imag[:, lanes] * wi
            sum_i = sum_i + real[:, lanes] * wi + imag[:, lanes] * wr
        for v in (sum_r, sum_i):
            v = v + pltpu.roll(v, 64, 1)
            totals.append(v + pltpu.roll(v, 32, 1))
    group = iota((MODES, 128), 1) // C
    r0, i0, r1, i1 = totals
    mixed = jnp.where(group == 0, r0, jnp.where(group == 1, i0, jnp.where(group == 2, r1, i1)))
    other = jnp.where(group == 0, -i0, jnp.where(group == 1, r0, jnp.where(group == 2, -i1, r1)))
    result = table_dot(back[...], jnp.concatenate([mixed, other], axis=0))
    out[...] = result.reshape(N_GX, CX, 128).astype(out.dtype)


def back_kernel(got, back, out):
    lines = [got[:, x, :].astype(F32) for x in range(CX)]
    group = iota((MODES, 128), 1) // C
    turned = []
    for g in range(4):
        line = jnp.zeros((MODES, 128), F32)
        for x in range(CX):
            shift = ((x - g) * C) % 128
            moved = lines[x] if shift == 0 else pltpu.roll(lines[x], shift, 1)
            line = jnp.where(group == x, moved, line)
        turned.append(line)
    r0, i0, r1, i1 = turned
    stack = jnp.concatenate(
        [jnp.concatenate(turned, axis=1), jnp.concatenate([-i0, r0, -i1, r1], axis=1)], axis=0
    )
    result = table_dot(back[...], stack)
    for g in range(4):
        piece = result[:, g * 128 : (g + 1) * 128].reshape(N_GY, CY, 128)
        out[:, g * CY : (g + 1) * CY, :] = piece.astype(out.dtype)


def end_kernel(got, inverse, known, out, wide):
    wide[...] = got[...].astype(F32).reshape(N_GY * 4 * CY, 128)
    for y in range(CY):
        values = wide[pl.ds(y, 4 * N_GY, stride=CY), :].astype(BF16)
        both = dot(values, inverse[...], TN)
        line = both[:, :NZ] + both[:, NZ:]
        for x in range(CX):
            h = line[x * C : (x + 1) * C] + known[x * CY + y]
            th = jnp.tanh(h * (GELU_B * (h * h) + GELU_A))
            out[x, y] = 0.5 * (h + h * th)


def call(kernel, out_shape, in_specs, scratch=(), flops=0, size=0, vmem=8 * 1024 * 1024):
    return pl.pallas_call(
        kernel,
        out_shape=out_shape,
        in_specs=in_specs,
        scratch_shapes=list(scratch),
        compiler_params=pltpu.CompilerParams(vmem_limit_bytes=vmem),
        cost_estimate=pl.CostEstimate(flops=flops, bytes_accessed=size, transcendentals=0),
    )


VM = pl.BlockSpec(memory_space=pltpu.VMEM)
SM = pl.BlockSpec(memory_space=pltpu.SMEM)


def stage_one(
    features, offsets, point_cell, tile_owner, tile_local, live_count,
    w_first, b_first, w_second, b_second, w_third, *_,
):
    forward_z = tables(CX * N_GX, CY * N_GY)[0]
    vm = pltpu.VMEM
    return call(
        pair_kernel,
        jax.ShapeDtypeStruct((N_GY, 16 + BLK * NZ // 4, 128), BF16),
        [SM, SM, SM] + [VM] * 9,
        [
            vm((PAIRS * NZ // 4, 4 * C), F32),
            vm((NZ // 4, 4 * HID), F32), vm((NZ // 4, 4 * HID), F32),
            vm((4 * HID, 4 * HID), F32), vm((4 * HID, 4 * C), F32),
            vm((8, 4 * HID), F32), vm((BLK, PB, PB), F32), vm((BLK, PB, PB), F32),
            vm((PB, PB), F32), vm((PB, PB), F32), vm((N_GY, 16, 128), F32),
        ],
        flops=1_600_000_000, size=1_000_000, vmem=VMEM_ONE,
    )(
        tile_owner, tile_local, live_count, features, offsets, point_cell.reshape(1, -1),
        w_first.T, b_first.reshape(1, -1), b_second.reshape(1, -1), w_second, w_third, forward_z,
    )


def local(
    features, offsets, point_cell, tile_owner, tile_local, live_count,
    w_first, b_first, w_second, b_second, w_third, w_point, b_point, w_modes,
):
    _, inverse_z, phase_y, back_y, forward_x, back_x = tables(CX * N_GX, CY * N_GY)
    vm = pltpu.VMEM
    sent = stage_one(
        features, offsets, point_cell, tile_owner, tile_local, live_count,
        w_first, b_first, w_second, b_second, w_third,
    )
    sent = lax.all_to_all(sent, "gy", 0, 0, tiled=True)
    along_y, slots = call(
        y_kernel,
        (jax.ShapeDtypeStruct((MODES, CX, 128), F32), jax.ShapeDtypeStruct((8, 128), jnp.int32)),
        [VM, VM],
        flops=100_000_000, size=500_000,
    )(sent, phase_y)
    known = call(
        tile_kernel,
        jax.ShapeDtypeStruct((CX * CY, C, NZ), F32),
        [SM] + [VM] * 3,
        [vm((CX * CY * NZ // 4, 4 * C), F32)],
        flops=100_000_000, size=2_500_000,
    )(slots, sent, w_point, b_point.reshape(C, 1))
    along_y = lax.all_to_all(along_y, "gx", 0, 0, tiled=True)
    along_y, known = lax.optimization_barrier((along_y, known))
    lines = call(
        x_kernel,
        jax.ShapeDtypeStruct((N_GX, CX, 128), F32),
        [VM] * 4,
        flops=100_000_000, size=500_000,
    )(along_y, w_modes.reshape(MODES, -1), forward_x, back_x)
    lines = lax.all_to_all(lines, "gx", 0, 0, tiled=True)
    cells = call(
        back_kernel,
        jax.ShapeDtypeStruct((N_GY, 4 * CY, 128), BF16),
        [VM] * 2,
        flops=100_000_000, size=500_000,
    )(lines, back_y)
    cells = lax.all_to_all(cells, "gy", 0, 0, tiled=True)
    return call(
        end_kernel,
        jax.ShapeDtypeStruct((CX, CY, C, NZ), F32),
        [VM] * 3,
        [vm((N_GY * 4 * CY, 128), F32)],
        flops=100_000_000, size=1_000_000,
    )(cells, inverse_z, known)


def solution(mesh):
    both = ("gx", "gy")
    return jax.shard_map(
        local,
        mesh=mesh,
        in_specs=(
            P(None, both), P(None, both), P(both), P(both, None), P(both, None), P(both),
            P(), P(), P(), P(), P(), P(), P(),
            P(None, "gx", "gy", None, None, None),
        ),
        out_specs=P("gx", "gy", None, None),
        check_vma=False,
    )
```
